256 devices in a mesh: section: 4 (over x), dp: 16 (over z, core), tensor: 4 (over y).
Axes of the slice: x: 4, y: 4, z: 8, core: 2. Of those that a mesh axis runs over, the one named last changes fastest.
Arguments:
- acts: bfloat16 [4, 4, 16, 128, 4096], P('section', None, 'dp', None, 'tensor'), may hold values from -24 to 24
- w_qkv: bfloat16 [4, 4096, 5120], P('section', None, 'tensor'), may hold values from -2 to 2
- lengths: int32 [4, 16, 4], replicated, may hold values from 1 to 383, as said below
- block_source: int32 [4, 64], replicated, may hold values from 0 to 63, as said below
Outputs:
- context: bfloat16 [4, 8192, 4096], P('section', 'dp', 'tensor')
The draws below stay inside these ranges and needn't reach their ends.
Inputs may be any that keep to these rules, and one draw needn't show every extreme that they name: `block_source`: for every section, each block of the sending order fills exactly one slot; the blocks of one document go to one replica; a replica takes at most 1 block held by any one index of dp, and exactly 1 from some index. The 4 lengths of each sequence sum to 512.
All inputs are finite; a program needn't handle non-finite values.
Results may differ from the reference program's by a relative error of at most 0.012.
The reference program's roundings to bfloat16 on the way (of `sent`, `received`, `normed`, `queries` and `probs_low`) count: a program that leaves them out, or rounds other values in their place, can miss the bound.
Values may be sent and summed in bfloat16 or wider, within the bound.
A program may use at most 128 MiB of HBM per device.

```python
import math
import jax
import jax.numpy as jnp
from jax import lax

D = 4096
HD = 128
HQ = 32
KV = 4
HB = 128
BLK = 128
DOCS = 4
TOK_DEV = 512
GQ = 8
COLS = 5120
NB = 4
SECTIONS = 4
WINDOWS = 16
SEQ = 8192
BLOCKS = 64
N_DP = 16


def draw_acts(key, part):
    key = jax.random.fold_in(key, 11)
    k_base, k_rough = jax.random.split(key, 2)
    dims_all = (SECTIONS, NB, N_DP, BLK, D)
    feature = jnp.arange(D, dtype=jnp.float32)
    ramp = jnp.exp(math.log(4.0) * feature / (D - 1)) * jax.random.uniform(k_rough, (D,), jnp.float32, 0.6, 1.5)
    values = jax.random.normal(k_base, dims_all, jnp.float32) * ramp
    return jnp.clip(values, -24.0, 24.0).astype(jnp.bfloat16)


def draw_w_qkv(key, part):
    key = jax.random.fold_in(key, 12)
    base = jax.random.normal(key, (SECTIONS, D, KV, GQ + 2, HD), jnp.float32) / math.sqrt(D)
    return jnp.clip(base, -2.0, 2.0).reshape(SECTIONS, D, COLS).astype(jnp.bfloat16)


def shared_layout(key):
    cut_key, head_key, tail_key = jax.random.split(key, 3)
    cut_shift = jax.random.randint(cut_key, (), 0, NB - 1, dtype=jnp.int32)
    section_ids = jnp.arange(SECTIONS, dtype=jnp.int32)
    cut_sizes = (1 + (section_ids + cut_shift) % (NB - 1)).astype(jnp.int32)
    head_tokens = (cut_sizes * BLK)[:, None]
    tail_tokens = ((NB - cut_sizes) * BLK)[:, None]
    head_first = jax.random.randint(head_key, (SECTIONS, WINDOWS), 1, head_tokens, dtype=jnp.int32)
    tail_first = jax.random.randint(tail_key, (SECTIONS, WINDOWS), 1, tail_tokens, dtype=jnp.int32)
    window_ids = jnp.arange(WINDOWS, dtype=jnp.int32)[None, :]
    head_first = jnp.where(window_ids == 0, head_tokens - 1, head_first)
    layout = jnp.stack([head_first, head_tokens - head_first, tail_first, tail_tokens - tail_first], axis=-1)
    return (layout.astype(jnp.int32), cut_sizes)


def plan_section(section_lengths, cut_size, section_key):
    head_cost = section_lengths[:, 0] * section_lengths[:, 0] + section_lengths[:, 1] * section_lengths[:, 1]
    tail_cost = section_lengths[:, 2] * section_lengths[:, 2] + section_lengths[:, 3] * section_lengths[:, 3]
    window_ids = jnp.arange(WINDOWS, dtype=jnp.int32)
    residue = window_ids * NB % WINDOWS
    same_class = residue[:, None] == residue[None, :]
    earlier = window_ids[None, :] < window_ids[:, None]
    head_before = (head_cost[None, :] > head_cost[:, None]) | (head_cost[None, :] == head_cost[:, None]) & earlier
    tail_before = (tail_cost[None, :] < tail_cost[:, None]) | (tail_cost[None, :] == tail_cost[:, None]) & earlier
    head_rank = jnp.sum((same_class & head_before).astype(jnp.int32), axis=1)
    tail_rank = jnp.sum((same_class & tail_before).astype(jnp.int32), axis=1)
    matched = same_class & (tail_rank[None, :] == head_rank[:, None])
    partner = jnp.sum(jnp.where(matched, window_ids[None, :], 0), axis=1).astype(jnp.int32)
    receiver_order = jax.random.permutation(section_key, WINDOWS).astype(jnp.int32)
    head_source = receiver_order
    tail_source = partner[receiver_order]
    slot_index = jnp.arange(NB, dtype=jnp.int32)[None, :]
    plan = jnp.where(slot_index < cut_size, head_source[:, None] * NB + slot_index, tail_source[:, None] * NB + slot_index)
    return plan.reshape(BLOCKS).astype(jnp.int32)


def draw_lengths(key, part):
    layout, cut_sizes = shared_layout(key)
    return layout


def draw_block_source(key, part):
    layout, cut_sizes = shared_layout(key)
    key = jax.random.fold_in(key, 13)
    section_keys = jax.random.split(key, SECTIONS)
    return jax.vmap(plan_section)(layout, cut_sizes, section_keys).astype(jnp.int32)


def setup_inputs(seed: int = 0) -> dict:
    key_list = jax.random.split(jax.random.key(seed), 5)
    acts = draw_acts(jax.random.fold_in(key_list[4], 71), 0)
    w_qkv = draw_w_qkv(jax.random.fold_in(key_list[4], 71), 0)
    lengths = draw_lengths(jax.random.fold_in(key_list[4], 71), 0)
    block_source = draw_block_source(jax.random.fold_in(key_list[4], 71), 0)
    return {"acts": acts, "w_qkv": w_qkv, "lengths": lengths, "block_source": block_source}


norm_eps = 1e-05
rope_theta = 500000.0

def hadamard(block_size):
    counter = jnp.arange(block_size, dtype=jnp.int32)
    shared_bits = jnp.bitwise_and(counter[:, None], counter[None, :])
    parity = jnp.zeros((block_size, block_size), jnp.int32)
    for bit_pos in range(block_size.bit_length()):
        parity = parity + jnp.bitwise_and(jnp.right_shift(shared_bits, bit_pos), 1)
    signs = jnp.where(parity % 2 == 0, 1.0, -1.0).astype(jnp.float32)
    return signs / math.sqrt(block_size)

def rotate_rows(values_in):
    dims_all = values_in.shape
    blocks = values_in.reshape(dims_all[:-1] + (dims_all[-1] // HB, HB))
    turned = jnp.einsum('...ij,jk->...ik', blocks, hadamard(HB), precision=lax.Precision.HIGHEST)
    return turned.reshape(dims_all)

def doc_layout(token_index, section_lengths):
    window = token_index // TOK_DEV
    offset = token_index % TOK_DEV
    doc_lengths = section_lengths[window]
    doc_ends = jnp.cumsum(doc_lengths, axis=-1)
    doc_index = lax.optimization_barrier(jnp.sum((offset[:, None] >= doc_ends).astype(jnp.int32), axis=-1))
    starts = doc_ends - doc_lengths
    which = jnp.arange(DOCS, dtype=jnp.int32)[None, :] == doc_index[:, None]
    chosen = lax.optimization_barrier(jnp.sum(jnp.where(which, starts, 0), axis=-1))
    return (window * DOCS + doc_index, offset - chosen)

def rotary(values_in, positions):
    half_dim = HD // 2
    steps_f = jnp.arange(half_dim, dtype=jnp.float32)
    inv_freq = jnp.exp(-math.log(rope_theta) * 2.0 * steps_f / HD)
    angles = positions.astype(jnp.float32)[:, None] * inv_freq[None, :]
    angles = angles.reshape((angles.shape[0],) + (1,) * (values_in.ndim - 2) + (half_dim,))
    cosine = jnp.cos(angles)
    sine_vals = jnp.sin(angles)
    first_half = values_in[..., :half_dim]
    second_half = values_in[..., half_dim:]
    return jnp.concatenate([first_half * cosine - second_half * sine_vals, second_half * cosine + first_half * sine_vals], axis=-1)

def reference(acts, w_qkv, lengths, block_source):
    score_scale = 1.0 / math.sqrt(HD)
    outputs = []
    for my_section in range(SECTIONS):
        source = acts[(my_section - 1) % SECTIONS].astype(jnp.float32)
        sent = rotate_rows(source).astype(jnp.bfloat16)
        ordered = sent.reshape(BLOCKS, BLK, D)
        route_plan = block_source[my_section]
        received = ordered[route_plan].reshape(SEQ, D)
        widened = received.astype(jnp.float32)
        square_mean = lax.optimization_barrier(jnp.mean(widened * widened, axis=-1, keepdims=True))
        normed = (widened * lax.rsqrt(square_mean + norm_eps)).astype(jnp.bfloat16)
        token_index = (route_plan[:, None] * BLK + jnp.arange(BLK, dtype=jnp.int32)[None, :]).reshape(SEQ).astype(jnp.int32)
        doc_ids, positions = doc_layout(token_index, lengths[my_section])
        weight_section = w_qkv[my_section]

        def replica(member):
            row_first = (member * TOK_DEV).astype(jnp.int32)
            row_block = lax.dynamic_slice_in_dim(normed, row_first, TOK_DEV, 0)
            row_ids = lax.dynamic_slice_in_dim(doc_ids, row_first, TOK_DEV, 0)
            row_pos = lax.dynamic_slice_in_dim(positions, row_first, TOK_DEV, 0)
            projected = jnp.dot(row_block, weight_section, preferred_element_type=jnp.float32)
            projected = projected.reshape(TOK_DEV, KV, GQ + 2, HD)
            queries = rotary(projected[:, :, :GQ], row_pos).astype(jnp.bfloat16)
            key_rows = rotary(projected[:, :, GQ], row_pos).astype(jnp.bfloat16)
            value_rows = projected[:, :, GQ + 1].astype(jnp.bfloat16)
            scores = jnp.einsum('rgqd,sgd->gqrs', queries.astype(jnp.float32), key_rows.astype(jnp.float32)) * score_scale
            seen = (row_ids[:, None] == row_ids[None, :]) & (row_pos[None, :] <= row_pos[:, None])
            row_max = lax.optimization_barrier(jnp.max(jnp.where(seen, scores, -1e+30), axis=-1, keepdims=True))
            probs = jnp.where(seen, jnp.exp(scores - row_max), 0.0)
            totals = lax.optimization_barrier(jnp.sum(probs, axis=-1))
            probs_low = probs.astype(jnp.bfloat16)
            context = jnp.einsum('gqrs,sgd->rgqd', probs_low.astype(jnp.float32), value_rows.astype(jnp.float32))
            context = context / jnp.transpose(totals, (2, 0, 1))[..., None]
            return context.reshape(TOK_DEV, HQ * HD).astype(jnp.bfloat16)
        section_out = lax.map(replica, jnp.arange(N_DP, dtype=jnp.int32))
        outputs.append(section_out.reshape(SEQ, HQ * HD))
    return jnp.stack(outputs)
```

```python
import functools
import math

import jax
import jax.numpy as jnp
from jax import lax
from jax.experimental import pallas as pl
from jax.experimental.pallas import tpu as pltpu
from jax.sharding import PartitionSpec as P

HD = 128
HB = 128
BLK = 128
DOCS = 4
TOK_DEV = 512
GQ = 8
NB = 4
D = 4096
LOCAL = 1024
COLS = 1280
CHIPS = 8
REPL = 16
CHUNKS = 4
FEAT = LOCAL // CHUNKS
HALF = FEAT // 2
ROWS = 16
AHEAD = 2

norm_eps = 1e-05
rope_theta = 500000.0
MESH = pl.DeviceIdType.MESH


def rotated_chip(step, chip):
    distance = CHIPS // 2 - (step + 1) // 2
    sign = 2 * (step % 2) - 1
    return (chip + CHIPS + sign * distance) % CHIPS


def slot_docs(bs_ref, len_ref, section, block, offset_iota):
    window = block // NB
    base = (section * REPL + window) * DOCS
    offset = (block % NB) * BLK + offset_iota
    end = len_ref[base]
    start = jnp.zeros_like(offset)
    document = jnp.zeros_like(offset)
    for d in range(DOCS):
        past = offset >= end
        document = document + past.astype(jnp.int32)
        start = jnp.where(past, end, start)
        if d < DOCS - 1:
            end = end + len_ref[base + d + 1]
    return window * DOCS + document, offset - start


def exchange_kernel(
    sections, tensors, acts_ref, w_ref, len_ref, bs_ref, qkv_ref,
    sbuf, obuf, x, wv, acc, squares, cos_t, sin_t,
    w_sem, p1_send, p1_recv, p2_send, p2_recv, y_send, y_recv, *mid
):
    s = lax.axis_index("section")
    i = lax.axis_index("dp")
    t = lax.axis_index("tensor")
    chip, core = i // 2, i % 2
    s_next = (s + 1) % sections
    s_prev = (s + sections - 1) % sections
    t_right = (t + 1) % tensors
    t_left = (t + tensors - 1) % tensors
    t_far = (t + 2) % tensors

    w_copy = pltpu.make_async_copy(w_ref, wv, w_sem)
    w_copy.start()

    barrier = pltpu.get_barrier_semaphore()

    def greet(q, carry):
        pl.semaphore_signal(barrier, inc=1, device_id=(s_prev, q, t), device_id_type=MESH)
        return carry

    def greet_peer(q, carry):
        peer = (i + q) % REPL
        pl.semaphore_signal(barrier, inc=1, device_id=(s, peer, t), device_id_type=MESH)
        return carry

    lax.fori_loop(0, REPL, greet, 0)
    lax.fori_loop(1, REPL, greet_peer, 0)
    pl.semaphore_signal(barrier, inc=1, device_id=(s, i, t_right), device_id_type=MESH)
    pl.semaphore_signal(barrier, inc=1, device_id=(s, i, t_left), device_id_type=MESH)

    row_id = lax.broadcasted_iota(jnp.int32, (2 * HB, 2 * HB), 0)
    col_id = lax.broadcasted_iota(jnp.int32, (2 * HB, 2 * HB), 1)
    shared = row_id & col_id & (HB - 1)
    shared = shared ^ (shared >> 4)
    shared = shared ^ (shared >> 2)
    shared = shared ^ (shared >> 1)
    sign = (1 - 2 * (shared & 1)).astype(jnp.float32)
    signs = jnp.where((row_id // HB) == (col_id // HB), sign, 0.0).astype(jnp.bfloat16)

    def rotate(c):
        for part in range(FEAT // (2 * HB)):
            first = c * FEAT + part * 2 * HB
            block_rows = acts_ref[:, :, first:first + 2 * HB].reshape(NB * BLK, 2 * HB)
            turned = jnp.dot(block_rows, signs, preferred_element_type=jnp.float32)
            low = (turned * (1.0 / math.sqrt(HB))).astype(jnp.bfloat16)
            for piece in range(2):
                column = part * 2 * HB + piece * HB
                h, inside = column // HALF, column % HALF
                values = low[:, piece * HB:(piece + 1) * HB].reshape(NB, CHIPS, ROWS, HB)
                for l in range(NB):
                    sbuf[c, h, :, l, :, inside:inside + HB] = values[l]

    def spread(c):
        def send(e, carry):
            to_chip = rotated_chip(e // 2, chip)
            to_core = (e + 1 + core) % 2
            pltpu.make_async_remote_copy(
                src_ref=sbuf.at[c, to_core, to_chip],
                dst_ref=mid[c].at[i],
                send_sem=p1_send.at[c],
                recv_sem=p1_recv.at[c],
                device_id=(s_next, to_chip * 2 + to_core, t),
                device_id_type=MESH,
            ).start()
            return carry

        lax.fori_loop(0, REPL, send, 0)

    def pick(c, j, k):
        block = bs_ref[s * (REPL * NB) + j * NB + k]
        return mid[c][block % REPL, block // REPL]

    def deliver(c):
        pltpu.make_async_copy(mid[c], mid[c], p1_recv.at[c]).wait()

        def send(e, carry):
            to_chip = rotated_chip(e // 2, chip)
            to_core = (e + 1 + core) % 2
            j = to_chip * 2 + to_core
            for k in range(NB):
                obuf[c, j, k] = pick(c, j, k)
            pltpu.make_async_remote_copy(
                src_ref=obuf.at[c, j],
                dst_ref=x.at[t, c, core, :, chip],
                send_sem=p2_send.at[c],
                recv_sem=p2_recv.at[c],
                device_id=(s, j, t),
                device_id_type=MESH,
            ).start()
            return carry

        lax.fori_loop(0, REPL - 1, send, 0)
        for k in range(NB):
            x[t, c, core, k, chip] = pick(c, i, k)

    def y_copy(way, c):
        view = [x.at[t, c], x.at[t, c], x.at[t_left, c, 0], x.at[t_right, c, 1]][way]
        return pltpu.make_async_remote_copy(
            src_ref=view, dst_ref=view, send_sem=y_send.at[way, c], recv_sem=y_recv.at[way, c],
            device_id=(s, i, t_left if way % 2 else t_right), device_id_type=MESH)

    def gather_start(c):
        pltpu.make_async_copy(
            obuf.at[c, pl.ds(0, REPL - 1)], obuf.at[c, pl.ds(0, REPL - 1)], p2_recv.at[c]).wait()
        y_copy(0, c).start()
        y_copy(1, c).start()

    def gather_forward(c):
        y_copy(0, c).wait_recv()
        y_copy(2, c).start()
        y_copy(1, c).wait_recv()
        y_copy(3, c).start()

    def gather_finish(c):
        y_copy(2, c).wait_recv()
        y_copy(3, c).wait_recv()

    def piece(u, c):
        halves = [x[u, c, h].reshape(NB * BLK, HALF) for h in range(2)]
        return jnp.concatenate(halves, axis=1)

    def multiply(pieces):
        rows_in = []
        for u, c in pieces:
            value = piece(u, c)
            rows_in.append(value)
            wide = value.astype(jnp.float32)
            wide = wide * wide
            total = wide[:, :HB]
            for g in range(1, FEAT // HB):
                total = total + wide[:, g * HB:(g + 1) * HB]
            squares[...] += total

        def tile(n, carry):
            columns = pl.ds(pl.multiple_of(n * 256, 256), 256)
            result = acc[:, columns]
            for (u, c), value in zip(pieces, rows_in):
                rows_w = pl.ds(pl.multiple_of(u * LOCAL + c * FEAT, FEAT), FEAT)
                result = result + jnp.dot(value, wv[rows_w, columns], preferred_element_type=jnp.float32)
            acc[:, columns] = result
            return carry

        lax.fori_loop(0, COLS // 256, tile, 0)

    rotate(0)
    pl.semaphore_wait(barrier, 2 * REPL + 1)
    spread(0)
    for c in range(1, CHUNKS):
        rotate(c)
        if c < AHEAD:
            spread(c)

    acc[...] = jnp.zeros_like(acc)
    squares[...] = jnp.zeros_like(squares)
    lane = lax.broadcasted_iota(jnp.int32, (BLK, HD), 1)
    row = lax.broadcasted_iota(jnp.int32, (BLK, HD), 0)
    steps_f = (lane % (HD // 2)).astype(jnp.float32)
    inv_freq = jnp.exp(-math.log(rope_theta) * 2.0 * steps_f / HD)
    for k in range(NB):
        block = bs_ref[s * (REPL * NB) + i * NB + k]
        _, position = slot_docs(bs_ref, len_ref, s, block, row)
        angles = position.astype(jnp.float32) * inv_freq
        sine = jnp.sin(angles)
        cos_t[k * BLK:(k + 1) * BLK] = jnp.cos(angles)
        sin_t[k * BLK:(k + 1) * BLK] = jnp.where(lane < HD // 2, -sine, sine)

    w_copy.wait()
    for c in range(CHUNKS + 3):
        if c < CHUNKS:
            deliver(c)
            if c + AHEAD < CHUNKS:
                spread(c + AHEAD)
        if 0 <= c - 1 < CHUNKS:
            gather_start(c - 1)
        if 0 <= c - 2 < CHUNKS:
            gather_forward(c - 2)
        pieces = []
        if 0 <= c - 2 < CHUNKS:
            pieces += [(t, c - 2), (t_left, c - 2), (t_right, c - 2)]
        if 0 <= c - 3 < CHUNKS - 1:
            gather_finish(c - 3)
            pieces += [(t_far, c - 3)]
        if c - 3 == CHUNKS - 1:
            gather_finish(c - 3)
            pieces += [(t_far, c - 3)]
        if pieces:
            multiply(pieces)

    mean = jnp.sum(squares[...], axis=1, keepdims=True) * (1.0 / D)
    scale = lax.rsqrt(mean + norm_eps)
    cosine = cos_t[...] * scale
    sine = sin_t[...] * scale
    for head in range(GQ + 1):
        values = acc[:, head * HD:(head + 1) * HD]
        swapped = pltpu.roll(values, HD // 2, 1)
        qkv_ref[:, head * HD:(head + 1) * HD] = (values * cosine + swapped * sine).astype(jnp.bfloat16)
    last = (GQ + 1) * HD
    qkv_ref[:, last:last + HD] = (acc[:, last:last + HD] * scale).astype(jnp.bfloat16)

    for c in range(CHUNKS):
        pltpu.make_async_copy(sbuf.at[c], sbuf.at[c], p1_send.at[c]).wait()
        pltpu.make_async_copy(
            obuf.at[c, pl.ds(0, REPL - 1)], obuf.at[c, pl.ds(0, REPL - 1)], p2_send.at[c]).wait()
        for way in range(4):
            y_copy(way, c).wait_send()


def attention_kernel(qkv_ref, len_ref, bs_ref, out_ref, bias):
    s = lax.axis_index("section")
    i = lax.axis_index("dp")
    blocks = [bs_ref[s * (REPL * NB) + i * NB + k] for k in range(NB)]
    across = lax.broadcasted_iota(jnp.int32, (1, BLK), 1)
    down = lax.broadcasted_iota(jnp.int32, (BLK, 1), 0)
    seen_by = [slot_docs(bs_ref, len_ref, s, block, across) for block in blocks]
    key_doc = jnp.concatenate([v[0] for v in seen_by], axis=1)
    key_pos = jnp.concatenate([v[1] for v in seen_by], axis=1)
    for k in range(NB):
        row_doc, row_pos = slot_docs(bs_ref, len_ref, s, blocks[k], down)
        seen = (row_doc == key_doc) & (key_pos <= row_pos)
        bias[k * BLK:(k + 1) * BLK] = jnp.where(seen, 0.0, -1e30)

    keys = qkv_ref[:, GQ * HD:(GQ + 1) * HD]
    values = qkv_ref[:, (GQ + 1) * HD:]
    factor = math.log2(math.e) / math.sqrt(HD)
    for head in range(GQ):
        for k in range(NB):
            rows = slice(k * BLK, (k + 1) * BLK)
            queries = qkv_ref[rows, head * HD:(head + 1) * HD]
            scores = lax.dot_general(
                queries, keys, (((1,), (1,)), ((), ())), preferred_element_type=jnp.float32)
            scores = scores + bias[rows]
            row_max = jnp.max(scores, axis=1, keepdims=True)
            probs = jnp.exp2((scores - row_max) * factor)
            totals = jnp.sum(probs, axis=1, keepdims=True)
            context = jnp.dot(probs.astype(jnp.bfloat16), values, preferred_element_type=jnp.float32)
            out_ref[rows, head * HD:(head + 1) * HD] = (context / totals).astype(jnp.bfloat16)


def local(sections, tensors, acts, w_qkv, lengths, block_source):
    rows = NB * BLK
    flat_lengths = lengths.reshape(-1)
    flat_source = block_source.reshape(-1)
    vmem = pl.BlockSpec(memory_space=pltpu.VMEM)
    smem = pl.BlockSpec(memory_space=pltpu.SMEM)
    qkv = pl.pallas_call(
        functools.partial(exchange_kernel, sections, tensors),
        out_shape=jax.ShapeDtypeStruct((rows, COLS), jnp.bfloat16),
        in_specs=[vmem, pl.BlockSpec(memory_space=pl.ANY), smem, smem],
        out_specs=vmem,
        scratch_shapes=[
            pltpu.VMEM((CHUNKS, 2, CHIPS, NB, ROWS, HALF), jnp.bfloat16),
            pltpu.VMEM((CHUNKS, REPL, NB, ROWS, HALF), jnp.bfloat16),
            pltpu.VMEM((4, CHUNKS, 2, NB, CHIPS, ROWS, HALF), jnp.bfloat16),
            pltpu.VMEM((D, COLS), jnp.bfloat16),
            pltpu.VMEM((rows, COLS), jnp.float32),
            pltpu.VMEM((rows, HB), jnp.float32),
            pltpu.VMEM((rows, HD), jnp.float32),
            pltpu.VMEM((rows, HD), jnp.float32),
            pltpu.SemaphoreType.DMA,
            pltpu.SemaphoreType.DMA((CHUNKS,)),
            pltpu.SemaphoreType.DMA((CHUNKS,)),
            pltpu.SemaphoreType.DMA((CHUNKS,)),
            pltpu.SemaphoreType.DMA((CHUNKS,)),
            pltpu.SemaphoreType.DMA((4, CHUNKS)),
            pltpu.SemaphoreType.DMA((4, CHUNKS)),
        ] + [pltpu.VMEM((REPL, NB, ROWS, HALF), jnp.bfloat16)] * CHUNKS,
        compiler_params=pltpu.CompilerParams(
            collective_id=0, has_side_effects=True, vmem_limit_bytes=48 * 1024 * 1024),
        cost_estimate=pl.CostEstimate(
            flops=2 * rows * D * COLS, bytes_accessed=D * COLS * 2 + rows * COLS * 4, transcendentals=0),
    )(acts[0, :, 0], w_qkv[0], flat_lengths, flat_source)
    context = pl.pallas_call(
        attention_kernel,
        out_shape=jax.ShapeDtypeStruct((rows, GQ * HD), jnp.bfloat16),
        in_specs=[vmem, smem, smem],
        out_specs=vmem,
        scratch_shapes=[pltpu.VMEM((rows, rows), jnp.float32)],
        compiler_params=pltpu.CompilerParams(vmem_limit_bytes=32 * 1024 * 1024),
        cost_estimate=pl.CostEstimate(
            flops=4 * GQ * rows * rows * HD, bytes_accessed=rows * COLS * 4, transcendentals=GQ * rows * rows),
    )(qkv, flat_lengths, flat_source)
    return context[None]


def solution(mesh):
    placed = (P("section", None, "dp", None, "tensor"), P("section", None, "tensor"), P(), P())
    return jax.shard_map(
        functools.partial(local, mesh.shape["section"], mesh.shape["tensor"]),
        mesh=mesh, in_specs=placed, out_specs=P("section", "dp", "tensor"), check_vma=False,
    )
```

```python
import functools
import math

import jax
import jax.numpy as jnp
from jax import lax
from jax.experimental import pallas as pl
from jax.experimental.pallas import tpu as pltpu
from jax.sharding import PartitionSpec as P

HD = 128
HB = 128
BLK = 128
DOCS = 4
TOK_DEV = 512
GQ = 8
NB = 4
D = 4096
LOCAL = 1024
COLS = 1280
CHIPS = 8
REPL = 16
CHUNKS = 4
FEAT = LOCAL // CHUNKS
HALF = FEAT // 2
ROWS = 16
AHEAD = 2
VMEM_BYTES = 48 * 1024 * 1024
GROUP = 8

norm_eps = 1e-05
rope_theta = 500000.0
MESH = pl.DeviceIdType.MESH


def far_first(step, chip, core):
    size = (step + 1) // 2
    offset = (1 - step % 2) * (CHIPS // 2 - size) - (step % 2) * (size % (CHIPS // 2))
    return (chip + CHIPS + (1 - 2 * core) * offset) % CHIPS


def near_first(step, chip, core):
    size = (step + 1) // 2
    offset = (2 * (step % 2) - 1) * size
    return (chip + CHIPS + (1 - 2 * core) * offset) % CHIPS


def slot_docs(bs_ref, len_ref, section, block, offset_iota):
    window = block // NB
    offset = (block % NB) * BLK + offset_iota
    end = len_ref[section, 0, window]
    start = jnp.zeros_like(offset)
    document = jnp.zeros_like(offset)
    for d in range(DOCS):
        past = offset >= end
        document = document + past.astype(jnp.int32)
        start = jnp.where(past, end, start)
        if d < DOCS - 1:
            end = end + len_ref[section, d + 1, window]
    return window * DOCS + document, offset - start


def exchange_kernel(
    sections, tensors, acts_ref, w_ref, len_ref, bs_ref, qkv_ref,
    rows_in, sbuf, obuf, x, wv, acc, squares, cos_t, sin_t,
    a_sem, w_sem, p1_send, p1_recv, p2_send, p2_recv, y_send, y_recv, *mid
):
    s = lax.axis_index("section")
    i = lax.axis_index("dp")
    t = lax.axis_index("tensor")
    chip, core = i // 2, i % 2
    s_next = (s + 1) % sections
    s_prev = (s + sections - 1) % sections
    t_right = (t + 1) % tensors
    t_left = (t + tensors - 1) % tensors
    t_far = (t + 2) % tensors

    def fetch(c):
        return pltpu.make_async_copy(
            acts_ref.at[:, :, pl.ds(c * FEAT, FEAT)], rows_in.at[c], a_sem.at[c])

    for c in range(CHUNKS):
        fetch(c).start()
    w_copy = pltpu.make_async_copy(w_ref, wv, w_sem)
    w_copy.start()

    barrier = pltpu.get_barrier_semaphore()

    def greet(q, carry):
        pl.semaphore_signal(barrier, inc=1, device_id=(s_prev, q, t), device_id_type=MESH)
        return carry

    def greet_peer(q, carry):
        peer = (i + q) % REPL
        pl.semaphore_signal(barrier, inc=1, device_id=(s, peer, t), device_id_type=MESH)
        return carry

    lax.fori_loop(0, REPL, greet, 0)
    lax.fori_loop(1, REPL, greet_peer, 0)
    pl.semaphore_signal(barrier, inc=1, device_id=(s, i, t_right), device_id_type=MESH)
    pl.semaphore_signal(barrier, inc=1, device_id=(s, i, t_left), device_id_type=MESH)

    row_id = lax.broadcasted_iota(jnp.int32, (2 * HB, 2 * HB), 0)
    col_id = lax.broadcasted_iota(jnp.int32, (2 * HB, 2 * HB), 1)
    shared = row_id & col_id & (HB - 1)
    shared = shared ^ (shared >> 4)
    shared = shared ^ (shared >> 2)
    shared = shared ^ (shared >> 1)
    sign = (1 - 2 * (shared & 1)).astype(jnp.float32)
    signs = jnp.where((row_id // HB) == (col_id // HB), sign, 0.0).astype(jnp.bfloat16)

    def rotate(c):
        fetch(c).wait()
        for part in range(FEAT // (2 * HB)):
            first = part * 2 * HB
            block_rows = rows_in[c, :, :, first:first + 2 * HB].reshape(NB * BLK, 2 * HB)
            turned = jnp.dot(block_rows, signs, preferred_element_type=jnp.float32)
            low = (turned * (1.0 / math.sqrt(HB))).astype(jnp.bfloat16)
            for piece in range(2):
                column = part * 2 * HB + piece * HB
                h, inside = column // HALF, column % HALF
                values = low[:, piece * HB:(piece + 1) * HB].reshape(NB, CHIPS, ROWS, HB)
                for l in range(NB):
                    sbuf[c, h, :, l, :, inside:inside + HB] = values[l]

    def spread(c):
        def send(e, carry):
            to_chip = far_first(e % CHIPS, chip, core)
            to_core = (e // CHIPS + 1 + core) % 2
            pltpu.make_async_remote_copy(
                src_ref=sbuf.at[c, to_core, to_chip],
                dst_ref=mid[c].at[i],
                send_sem=p1_send.at[c],
                recv_sem=p1_recv.at[c],
                device_id=(s_next, to_chip * 2 + to_core, t),
                device_id_type=MESH,
            ).start()
            return carry

        lax.fori_loop(0, REPL, send, 0)

    def pick(c, j, k):
        block = bs_ref[s, j * NB + k]
        return mid[c][block % REPL, block // REPL]

    def deliver(c):
        pltpu.make_async_copy(mid[c], mid[c], p1_recv.at[c]).wait()

        def send(e, carry):
            to_chip = near_first(e // 2, chip, core)
            to_core = (e + core) % 2
            j = to_chip * 2 + to_core
            for k in range(NB):
                obuf[c, j, k] = pick(c, j, k)
            pltpu.make_async_remote_copy(
                src_ref=obuf.at[c, j],
                dst_ref=x.at[t, c, core, :, chip],
                send_sem=p2_send.at[c],
                recv_sem=p2_recv.at[c],
                device_id=(s, j, t),
                device_id_type=MESH,
            ).start()
            return carry

        lax.fori_loop(1, REPL, send, 0)
        for k in range(NB):
            x[t, c, core, k, chip] = pick(c, i, k)

    def y_copy(way, c):
        to_left, turn = way % 2, way // 2
        owner = t if turn < 2 else (t_right if to_left else t_left)
        half = (turn + to_left) % 2
        view = x.at[owner, c, half]
        return pltpu.make_async_remote_copy(
            src_ref=view, dst_ref=view, send_sem=y_send.at[way, c], recv_sem=y_recv.at[way, c],
            device_id=(s, i, t_left if to_left else t_right), device_id_type=MESH)

    def gather_start(c):
        pltpu.make_async_copy(
            obuf.at[c, pl.ds(0, REPL - 1)], obuf.at[c, pl.ds(0, REPL - 1)], p2_recv.at[c]).wait()
        for way in range(4):
            y_copy(way, c).start()

    def gather_forward(c):
        for way in range(2):
            y_copy(way, c).wait_recv()
            y_copy(way + 4, c).start()

    def gather_near(c):
        for way in range(2, 4):
            y_copy(way, c).wait_recv()

    def gather_finish(c):
        for way in range(4, 6):
            y_copy(way, c).wait_recv()

    def piece(u, c):
        halves = [x[u, c, h].reshape(NB * BLK, HALF) for h in range(2)]
        return jnp.concatenate(halves, axis=1)

    def multiply(pieces):
        rows_in = []
        for u, c in pieces:
            value = piece(u, c)
            rows_in.append(value)
            wide = value.astype(jnp.float32)
            wide = wide * wide
            total = wide[:, :HB]
            for g in range(1, FEAT // HB):
                total = total + wide[:, g * HB:(g + 1) * HB]
            squares[...] += total

        def tile(n, carry):
            columns = pl.ds(pl.multiple_of(n * 256, 256), 256)
            result = acc[:, columns]
            for (u, c), value in zip(pieces, rows_in):
                rows_w = pl.ds(pl.multiple_of(u * LOCAL + c * FEAT, FEAT), FEAT)
                result = result + jnp.dot(value, wv[rows_w, columns], preferred_element_type=jnp.float32)
            acc[:, columns] = result
            return carry

        lax.fori_loop(0, COLS // 256, tile, 0)

    rotate(0)
    pl.semaphore_wait(barrier, 2 * REPL + 1)
    spread(0)
    for c in range(1, CHUNKS):
        rotate(c)
        if c < AHEAD:
            spread(c)

    acc[...] = jnp.zeros_like(acc)
    squares[...] = jnp.zeros_like(squares)
    lane = lax.broadcasted_iota(jnp.int32, (BLK, HD), 1)
    row = lax.broadcasted_iota(jnp.int32, (BLK, HD), 0)
    steps_f = (lane % (HD // 2)).astype(jnp.float32)
    inv_freq = jnp.exp(-math.log(rope_theta) * 2.0 * steps_f / HD)
    for k in range(NB):
        block = bs_ref[s, i * NB + k]
        _, position = slot_docs(bs_ref, len_ref, s, block, row)
        angles = position.astype(jnp.float32) * inv_freq
        sine = jnp.sin(angles)
        cos_t[k * BLK:(k + 1) * BLK] = jnp.cos(angles)
        sin_t[k * BLK:(k + 1) * BLK] = jnp.where(lane < HD // 2, -sine, sine)

    w_copy.wait()
    for c in range(CHUNKS + 2):
        if c < CHUNKS:
            deliver(c)
            if c + AHEAD < CHUNKS:
                spread(c + AHEAD)
        if c >= 2:
            gather_forward(c - 2)
            gather_near(c - 2)
            multiply([(t, c - 2), (t_left, c - 2), (t_right, c - 2)])
            gather_finish(c - 2)
            multiply([(t_far, c - 2)])
        if 0 <= c - 1 < CHUNKS:
            gather_start(c - 1)

    mean = jnp.sum(squares[...], axis=1, keepdims=True) * (1.0 / D)
    scale = lax.rsqrt(mean + norm_eps)
    cosine = cos_t[...] * scale
    sine = sin_t[...] * scale
    for head in range(GQ + 1):
        values = acc[:, head * HD:(head + 1) * HD]
        swapped = pltpu.roll(values, HD // 2, 1)
        qkv_ref[:, head * HD:(head + 1) * HD] = (values * cosine + swapped * sine).astype(jnp.bfloat16)
    last = (GQ + 1) * HD
    qkv_ref[:, last:last + HD] = (acc[:, last:last + HD] * scale).astype(jnp.bfloat16)

    for c in range(CHUNKS):
        pltpu.make_async_copy(sbuf.at[c], sbuf.at[c], p1_send.at[c]).wait()
        pltpu.make_async_copy(
            obuf.at[c, pl.ds(0, REPL - 1)], obuf.at[c, pl.ds(0, REPL - 1)], p2_send.at[c]).wait()
        for way in range(6):
            y_copy(way, c).wait_send()


def attention_kernel(qkv_ref, len_ref, bs_ref, out_ref, keys, values, context, out_sem):
    s = lax.axis_index("section")
    i = lax.axis_index("dp")
    blocks = [bs_ref[s, i * NB + k] for k in range(NB)]
    ranks = [sum((other < block).astype(jnp.int32) for other in blocks) for block in blocks]
    slots = [sum(k * (ranks[k] == r).astype(jnp.int32) for k in range(NB)) for r in range(NB)]
    ordered = [sum(blocks[k] * (ranks[k] == r).astype(jnp.int32) for k in range(NB)) for r in range(NB)]
    across = lax.broadcasted_iota(jnp.int32, (1, BLK), 1)
    down = lax.broadcasted_iota(jnp.int32, (BLK, 1), 0)
    key_docs = [slot_docs(bs_ref, len_ref, s, block, across) for block in ordered]
    slot_rows = [pl.ds(pl.multiple_of(slot * BLK, BLK), BLK) for slot in slots]
    for r in range(NB):
        keys[:, r * BLK:(r + 1) * BLK] = qkv_ref[slot_rows[r], GQ * HD:(GQ + 1) * HD].T
        values[r * BLK:(r + 1) * BLK] = qkv_ref[slot_rows[r], (GQ + 1) * HD:]
    factor = math.log2(math.e) / math.sqrt(HD)

    def attend(r, first):
        row_doc, row_pos = slot_docs(bs_ref, len_ref, s, ordered[r], down)
        key_doc = jnp.concatenate([key_docs[f][0] for f in range(first, r + 1)], axis=1)
        key_pos = jnp.concatenate([key_docs[f][1] for f in range(first, r + 1)], axis=1)
        seen = (row_doc == key_doc) & (key_pos <= row_pos)
        near = slice(first * BLK, (r + 1) * BLK)
        near_keys, near_values = keys[:, near], values[near]
        for head in range(0, GQ, GROUP):
            group = range(head, head + GROUP)
            scores = [
                jnp.dot(qkv_ref[slot_rows[r], h * HD:(h + 1) * HD], near_keys, preferred_element_type=jnp.float32)
                for h in group
            ]
            scores = [jnp.where(seen, value, -1e30) for value in scores]
            row_max = [jnp.max(value, axis=1, keepdims=True) for value in scores]
            probs = [jnp.exp2((value - top) * factor) for value, top in zip(scores, row_max)]
            totals = [jnp.sum(value, axis=1, keepdims=True) for value in probs]
            sums = [
                jnp.dot(value.astype(jnp.bfloat16), near_values, preferred_element_type=jnp.float32)
                for value in probs
            ]
            for h, value, total in zip(group, sums, totals):
                context[r, :, h * HD:(h + 1) * HD] = (value / total).astype(jnp.bfloat16)

    copies = []
    for r in range(NB):
        same = [(ordered[f] // NB == ordered[r] // NB).astype(jnp.int32) for f in range(r)]
        count = sum(same) if same else jnp.int32(0)
        for earlier in range(r + 1):
            pl.when(count == earlier)(functools.partial(attend, r, r - earlier))
        copies.append(pltpu.make_async_copy(context.at[r], out_ref.at[slot_rows[r]], out_sem.at[r]))
        copies[r].start()
    for copy in copies:
        copy.wait()


def attention(qkv, by_document, block_source):
    rows = NB * BLK
    vmem = pl.BlockSpec(memory_space=pltpu.VMEM)
    smem = pl.BlockSpec(memory_space=pltpu.SMEM)
    return pl.pallas_call(
        attention_kernel,
        out_shape=jax.ShapeDtypeStruct((rows, GQ * HD), jnp.bfloat16),
        in_specs=[vmem, smem, smem],
        out_specs=pl.BlockSpec(memory_space=pl.ANY),
        scratch_shapes=[
            pltpu.VMEM((HD, rows), jnp.bfloat16),
            pltpu.VMEM((rows, HD), jnp.bfloat16),
            pltpu.VMEM((NB, BLK, GQ * HD), jnp.bfloat16),
            pltpu.SemaphoreType.DMA((NB,)),
        ],
        compiler_params=pltpu.CompilerParams(vmem_limit_bytes=32 * 1024 * 1024),
        cost_estimate=pl.CostEstimate(
            flops=4 * GQ * rows * rows * HD, bytes_accessed=rows * COLS * 4, transcendentals=GQ * rows * rows),
    )(qkv, by_document, block_source)


def local(sections, tensors, acts, w_qkv, lengths, block_source):
    rows = NB * BLK
    by_document = lengths.transpose(0, 2, 1)
    vmem = pl.BlockSpec(memory_space=pltpu.VMEM)
    smem = pl.BlockSpec(memory_space=pltpu.SMEM)
    qkv = pl.pallas_call(
        functools.partial(exchange_kernel, sections, tensors),
        out_shape=jax.ShapeDtypeStruct((rows, COLS), jnp.bfloat16),
        in_specs=[pl.BlockSpec(memory_space=pltpu.HBM)] * 2 + [smem] * 2,
        out_specs=vmem,
        scratch_shapes=[
            pltpu.VMEM((CHUNKS, NB, BLK, FEAT), jnp.bfloat16),
            pltpu.VMEM((CHUNKS, 2, CHIPS, NB, ROWS, HALF), jnp.bfloat16),
            pltpu.VMEM((CHUNKS, REPL, NB, ROWS, HALF), jnp.bfloat16),
            pltpu.VMEM((4, CHUNKS, 2, NB, CHIPS, ROWS, HALF), jnp.bfloat16),
            pltpu.VMEM((D, COLS), jnp.bfloat16),
            pltpu.VMEM((rows, COLS), jnp.float32),
            pltpu.VMEM((rows, HB), jnp.float32),
            pltpu.VMEM((rows, HD), jnp.float32),
            pltpu.VMEM((rows, HD), jnp.float32),
            pltpu.SemaphoreType.DMA((CHUNKS,)),
            pltpu.SemaphoreType.DMA,
            pltpu.SemaphoreType.DMA((CHUNKS,)),
            pltpu.SemaphoreType.DMA((CHUNKS,)),
            pltpu.SemaphoreType.DMA((CHUNKS,)),
            pltpu.SemaphoreType.DMA((CHUNKS,)),
            pltpu.SemaphoreType.DMA((6, CHUNKS)),
            pltpu.SemaphoreType.DMA((6, CHUNKS)),
        ] + [pltpu.VMEM((REPL, NB, ROWS, HALF), jnp.bfloat16)] * CHUNKS,
        compiler_params=pltpu.CompilerParams(
            collective_id=0, has_side_effects=True, vmem_limit_bytes=VMEM_BYTES),
        cost_estimate=pl.CostEstimate(
            flops=2 * rows * D * COLS, bytes_accessed=D * COLS * 2 + rows * COLS * 4, transcendentals=0),
    )(acts[0, :, 0], w_qkv[0], by_document, block_source)
    return attention(qkv, by_document, block_source)[None]


def solution(mesh):
    placed = (P("section", None, "dp", None, "tensor"), P("section", None, "tensor"), P(), P())
    return jax.shard_map(
        functools.partial(local, mesh.shape["section"], mesh.shape["tensor"]),
        mesh=mesh, in_specs=placed, out_specs=P("section", "dp", "tensor"), check_vma=False,
    )
```

```python
import functools
import math

import jax
import jax.numpy as jnp
from jax import lax
from jax.experimental import pallas as pl
from jax.experimental.pallas import tpu as pltpu
from jax.sharding import PartitionSpec as P

HD = 128
HB = 128
BLK = 128
DOCS = 4
TOK_DEV = 512
GQ = 8
NB = 4
D = 4096
LOCAL = 1024
COLS = 1280
CHIPS = 8
REPL = 16
CHUNKS = 4
FEAT = LOCAL // CHUNKS
HALF = FEAT // 2
ROWS = 16
AHEAD = 2
EARLY = 1
SPLIT = 1
SLOTS = NB // SPLIT
VMEM_BYTES = 48 * 1024 * 1024
GROUP = 8

norm_eps = 1e-05
rope_theta = 500000.0
MESH = pl.DeviceIdType.MESH


def far_first(step, chip, core):
    size = (step + 1) // 2
    offset = (1 - step % 2) * (CHIPS // 2 - size) - (step % 2) * (size % (CHIPS // 2))
    return (chip + CHIPS + (1 - 2 * core) * offset) % CHIPS


def slot_docs(bs_ref, len_ref, section, block, offset_iota):
    window = block // NB
    offset = (block % NB) * BLK + offset_iota
    end = len_ref[section, 0, window]
    start = jnp.zeros_like(offset)
    document = jnp.zeros_like(offset)
    for d in range(DOCS):
        past = offset >= end
        document = document + past.astype(jnp.int32)
        start = jnp.where(past, end, start)
        if d < DOCS - 1:
            end = end + len_ref[section, d + 1, window]
    return window * DOCS + document, offset - start


def exchange_kernel(
    sections, tensors, acts_ref, w_ref, len_ref, bs_ref, qkv_ref,
    rows_in, sbuf, obuf, x, wv, acc, squares, cos_t, sin_t,
    a_sem, w_sem, p1_send, p1_recv, p2_send, p2_recv, y_send, y_recv, *mid
):
    s = lax.axis_index("section")
    i = lax.axis_index("dp")
    t = lax.axis_index("tensor")
    chip, core = i // 2, i % 2
    s_next = (s + 1) % sections
    s_prev = (s + sections - 1) % sections
    t_right = (t + 1) % tensors
    t_left = (t + tensors - 1) % tensors
    t_far = (t + 2) % tensors

    def fetch(c):
        return pltpu.make_async_copy(
            acts_ref.at[:, :, pl.ds(c * FEAT, FEAT)], rows_in.at[c], a_sem.at[c])

    for c in range(CHUNKS):
        fetch(c).start()
    w_copy = pltpu.make_async_copy(w_ref, wv, w_sem)
    w_copy.start()

    barrier = pltpu.get_barrier_semaphore()

    def greet(q, carry):
        pl.semaphore_signal(barrier, inc=1, device_id=(s_prev, q, t), device_id_type=MESH)
        return carry

    def greet_peer(q, carry):
        peer = (i + q) % REPL
        pl.semaphore_signal(barrier, inc=1, device_id=(s, peer, t), device_id_type=MESH)
        return carry

    lax.fori_loop(0, REPL, greet, 0)
    lax.fori_loop(1, REPL, greet_peer, 0)
    pl.semaphore_signal(barrier, inc=1, device_id=(s, i, t_right), device_id_type=MESH)
    pl.semaphore_signal(barrier, inc=1, device_id=(s, i, t_left), device_id_type=MESH)

    row_id = lax.broadcasted_iota(jnp.int32, (2 * HB, 2 * HB), 0)
    col_id = lax.broadcasted_iota(jnp.int32, (2 * HB, 2 * HB), 1)
    shared = row_id & col_id & (HB - 1)
    shared = shared ^ (shared >> 4)
    shared = shared ^ (shared >> 2)
    shared = shared ^ (shared >> 1)
    sign = (1 - 2 * (shared & 1)).astype(jnp.float32)
    signs = jnp.where((row_id // HB) == (col_id // HB), sign, 0.0).astype(jnp.bfloat16)

    def rotate(c):
        fetch(c).wait()
        for part in range(FEAT // (2 * HB)):
            first = part * 2 * HB
            block_rows = rows_in[c, :, :, first:first + 2 * HB].reshape(NB * BLK, 2 * HB)
            turned = jnp.dot(block_rows, signs, preferred_element_type=jnp.float32)
            low = (turned * (1.0 / math.sqrt(HB))).astype(jnp.bfloat16)
            for piece in range(2):
                column = part * 2 * HB + piece * HB
                h, inside = column // HALF, column % HALF
                values = low[:, piece * HB:(piece + 1) * HB].reshape(NB, CHIPS, ROWS, HB)
                for l in range(NB):
                    sbuf[c, h, :, l, :, inside:inside + HB] = values[l]

    def spread(c):
        def send(e, carry):
            to_chip = far_first(e % CHIPS, chip, core)
            to_core = (e // CHIPS + 1 + core) % 2
            pltpu.make_async_remote_copy(
                src_ref=sbuf.at[c, to_core, to_chip],
                dst_ref=mid[c].at[i],
                send_sem=p1_send.at[c],
                recv_sem=p1_recv.at[c],
                device_id=(s_next, to_chip * 2 + to_core, t),
                device_id_type=MESH,
            ).start()
            return carry

        lax.fori_loop(0, REPL, send, 0)

    def pick(c, j, k):
        block = bs_ref[s, j * NB + k]
        return mid[c][block % REPL, block // REPL]

    def deliver(c):
        pltpu.make_async_copy(mid[c], mid[c], p1_recv.at[c]).wait()

        for part in range(SPLIT):
            slots = range(part * SLOTS, (part + 1) * SLOTS)

            def send(e, carry):
                to_chip = far_first((e - 1) % CHIPS, chip, core)
                to_core = ((e - 1) // CHIPS + 1 + core) % 2
                j = to_chip * 2 + to_core
                for k in slots:
                    obuf[c, part, j, k % SLOTS] = pick(c, j, k)
                pltpu.make_async_remote_copy(
                    src_ref=obuf.at[c, part, j],
                    dst_ref=x.at[t, c, part, core, chip],
                    send_sem=p2_send.at[c, part],
                    recv_sem=p2_recv.at[c, part],
                    device_id=(s, j, t),
                    device_id_type=MESH,
                ).start()
                return carry

            lax.fori_loop(1, REPL, send, 0)
            for k in slots:
                x[t, c, part, core, chip, k % SLOTS] = pick(c, i, k)

    def delivered(c, part, sem):
        view = obuf.at[c, part, pl.ds(0, REPL - 1)]
        return pltpu.make_async_copy(view, view, sem.at[c, part])

    def y_copy(way, c, part):
        to_left, turn = way % 2, way // 2
        owner = t if turn < 2 else (t_right if to_left else t_left)
        half = (turn + to_left) % 2
        view = x.at[owner, c, part, half]
        return pltpu.make_async_remote_copy(
            src_ref=view, dst_ref=view, send_sem=y_send.at[way, c, part], recv_sem=y_recv.at[way, c, part],
            device_id=(s, i, t_left if to_left else t_right), device_id_type=MESH)

    def gather_start(c, part):
        delivered(c, part, p2_recv).wait()
        for way in range(4):
            y_copy(way, c, part).start()

    def gather_forward(c, part):
        for way in range(2):
            y_copy(way, c, part).wait_recv()
            y_copy(way + 4, c, part).start()

    def gather_near(c, part):
        for way in range(2, 4):
            y_copy(way, c, part).wait_recv()

    def gather_far(c, part):
        for way in range(4, 6):
            y_copy(way, c, part).wait_recv()

    def piece(u, c, part):
        halves = [x[u, c, part, h].reshape(SLOTS * BLK, HALF) for h in range(2)]
        return jnp.concatenate(halves, axis=1)

    def multiply(c, part, owners):
        rows = pl.ds(part * SLOTS * BLK, SLOTS * BLK)
        pieces = [piece(u, c, part) for u in owners]
        for value in pieces:
            wide = value.astype(jnp.float32)
            wide = wide * wide
            total = wide[:, :HB]
            for g in range(1, FEAT // HB):
                total = total + wide[:, g * HB:(g + 1) * HB]
            squares[rows] += total

        def tile(n, carry):
            columns = pl.ds(pl.multiple_of(n * 256, 256), 256)
            result = acc[rows, columns]
            for u, value in zip(owners, pieces):
                rows_w = pl.ds(pl.multiple_of(u * LOCAL + c * FEAT, FEAT), FEAT)
                result = result + jnp.dot(value, wv[rows_w, columns], preferred_element_type=jnp.float32)
            acc[rows, columns] = result
            return carry

        lax.fori_loop(0, COLS // 256, tile, 0)

    def project(c, part):
        gather_near(c, part)
        gather_far(c, part)
        multiply(c, part, [t, t_left, t_right, t_far])

    def finish(part):
        rows = pl.ds(part * SLOTS * BLK, SLOTS * BLK)
        mean = jnp.sum(squares[rows], axis=1, keepdims=True) * (1.0 / D)
        scale = lax.rsqrt(mean + norm_eps)
        cosine = cos_t[part].reshape(SLOTS * BLK, HD) * scale
        sine = sin_t[part].reshape(SLOTS * BLK, HD) * scale

        def put(head, result):
            low = result.astype(jnp.bfloat16).reshape(CHIPS, SLOTS, ROWS, HD)
            for k in range(SLOTS):
                first = (part * SLOTS + k) * BLK
                qkv_ref[first:first + BLK, head * HD:(head + 1) * HD] = low[:, k].reshape(BLK, HD)

        for head in range(GQ + 1):
            values = acc[rows, head * HD:(head + 1) * HD]
            swapped = pltpu.roll(values, HD // 2, 1)
            put(head, values * cosine + swapped * sine)
        last = (GQ + 1) * HD
        put(GQ + 1, acc[rows, last:last + HD] * scale)

    rotate(0)
    pl.semaphore_wait(barrier, 2 * REPL + 1)
    spread(0)
    for c in range(1, CHUNKS):
        rotate(c)
        if c < AHEAD:
            spread(c)

    acc[...] = jnp.zeros_like(acc)
    squares[...] = jnp.zeros_like(squares)
    lane = lax.broadcasted_iota(jnp.int32, (BLK, HD), 1)
    row = lax.broadcasted_iota(jnp.int32, (BLK, HD), 0)
    steps_f = (lane % (HD // 2)).astype(jnp.float32)
    inv_freq = jnp.exp(-math.log(rope_theta) * 2.0 * steps_f / HD)
    for k in range(NB):
        block = bs_ref[s, i * NB + k]
        _, position = slot_docs(bs_ref, len_ref, s, block, row)
        angles = position.astype(jnp.float32) * inv_freq
        sine = jnp.sin(angles)
        sine = jnp.where(lane < HD // 2, -sine, sine)
        cos_t[k // SLOTS, :, k % SLOTS] = jnp.cos(angles).reshape(CHIPS, ROWS, HD)
        sin_t[k // SLOTS, :, k % SLOTS] = sine.reshape(CHIPS, ROWS, HD)

    w_copy.wait()
    for c in range(AHEAD):
        deliver(c)
        spread(c + AHEAD)
    waiting = []
    for c in range(CHUNKS):
        for part in range(SPLIT):
            gather_start(c, part)
            if c >= CHUNKS - AHEAD and len(waiting) > 1:
                project(*waiting.pop(0))
            gather_forward(c, part)
            waiting.append((c, part))
        if c + AHEAD < CHUNKS:
            deliver(c + AHEAD)
            while len(waiting) > EARLY:
                project(*waiting.pop(0))
    while len(waiting) > 1:
        project(*waiting.pop(0))
    for part in range(SPLIT - 1):
        finish(part)
    c, part = waiting[0]
    gather_near(c, part)
    multiply(c, part, [t, t_left, t_right])
    gather_far(c, part)
    multiply(c, part, [t_far])
    finish(part)

    for c in range(CHUNKS):
        pltpu.make_async_copy(sbuf.at[c], sbuf.at[c], p1_send.at[c]).wait()
        for part in range(SPLIT):
            delivered(c, part, p2_send).wait()
            for way in range(6):
                y_copy(way, c, part).wait_send()


def attention_kernel(qkv_ref, len_ref, bs_ref, out_ref, keys, values, context, out_sem):
    s = lax.axis_index("section")
    i = lax.axis_index("dp")
    blocks = [bs_ref[s, i * NB + k] for k in range(NB)]
    ranks = [sum((other < block).astype(jnp.int32) for other in blocks) for block in blocks]
    slots = [sum(k * (ranks[k] == r).astype(jnp.int32) for k in range(NB)) for r in range(NB)]
    ordered = [sum(blocks[k] * (ranks[k] == r).astype(jnp.int32) for k in range(NB)) for r in range(NB)]
    across = lax.broadcasted_iota(jnp.int32, (1, BLK), 1)
    down = lax.broadcasted_iota(jnp.int32, (BLK, 1), 0)
    key_docs = [slot_docs(bs_ref, len_ref, s, block, across) for block in ordered]
    slot_rows = [pl.ds(pl.multiple_of(slot * BLK, BLK), BLK) for slot in slots]
    for r in range(NB):
        keys[:, r * BLK:(r + 1) * BLK] = qkv_ref[slot_rows[r], GQ * HD:(GQ + 1) * HD].T
        values[r * BLK:(r + 1) * BLK] = qkv_ref[slot_rows[r], (GQ + 1) * HD:]
    factor = math.log2(math.e) / math.sqrt(HD)

    def attend(r, first):
        row_doc, row_pos = slot_docs(bs_ref, len_ref, s, ordered[r], down)
        key_doc = jnp.concatenate([key_docs[f][0] for f in range(first, r + 1)], axis=1)
        key_pos = jnp.concatenate([key_docs[f][1] for f in range(first, r + 1)], axis=1)
        seen = (row_doc == key_doc) & (key_pos <= row_pos)
        near = slice(first * BLK, (r + 1) * BLK)
        near_keys, near_values = keys[:, near], values[near]
        for head in range(0, GQ, GROUP):
            group = range(head, head + GROUP)
            scores = [
                jnp.dot(qkv_ref[slot_rows[r], h * HD:(h + 1) * HD], near_keys, preferred_element_type=jnp.float32)
                for h in group
            ]
            scores = [jnp.where(seen, value, -1e30) for value in scores]
            row_max = [jnp.max(value, axis=1, keepdims=True) for value in scores]
            probs = [jnp.exp2((value - top) * factor) for value, top in zip(scores, row_max)]
            totals = [jnp.sum(value, axis=1, keepdims=True) for value in probs]
            sums = [
                jnp.dot(value.astype(jnp.bfloat16), near_values, preferred_element_type=jnp.float32)
                for value in probs
            ]
            for h, value, total in zip(group, sums, totals):
                context[r, :, h * HD:(h + 1) * HD] = (value / total).astype(jnp.bfloat16)

    copies = []
    for r in range(NB):
        same = [(ordered[f] // NB == ordered[r] // NB).astype(jnp.int32) for f in range(r)]
        count = sum(same) if same else jnp.int32(0)
        for earlier in range(r + 1):
            pl.when(count == earlier)(functools.partial(attend, r, r - earlier))
        copies.append(pltpu.make_async_copy(context.at[r], out_ref.at[slot_rows[r]], out_sem.at[r]))
        copies[r].start()
    for copy in copies:
        copy.wait()


def attention(qkv, by_document, block_source):
    rows = NB * BLK
    vmem = pl.BlockSpec(memory_space=pltpu.VMEM)
    smem = pl.BlockSpec(memory_space=pltpu.SMEM)
    return pl.pallas_call(
        attention_kernel,
        out_shape=jax.ShapeDtypeStruct((rows, GQ * HD), jnp.bfloat16),
        in_specs=[vmem, smem, smem],
        out_specs=pl.BlockSpec(memory_space=pl.ANY),
        scratch_shapes=[
            pltpu.VMEM((HD, rows), jnp.bfloat16),
            pltpu.VMEM((rows, HD), jnp.bfloat16),
            pltpu.VMEM((NB, BLK, GQ * HD), jnp.bfloat16),
            pltpu.SemaphoreType.DMA((NB,)),
        ],
        compiler_params=pltpu.CompilerParams(vmem_limit_bytes=32 * 1024 * 1024),
        cost_estimate=pl.CostEstimate(
            flops=4 * GQ * rows * rows * HD, bytes_accessed=rows * COLS * 4, transcendentals=GQ * rows * rows),
    )(qkv, by_document, block_source)


def local(sections, tensors, acts, w_qkv, lengths, block_source):
    rows = NB * BLK
    by_document = lengths.transpose(0, 2, 1)
    vmem = pl.BlockSpec(memory_space=pltpu.VMEM)
    smem = pl.BlockSpec(memory_space=pltpu.SMEM)
    qkv = pl.pallas_call(
        functools.partial(exchange_kernel, sections, tensors),
        out_shape=jax.ShapeDtypeStruct((rows, COLS), jnp.bfloat16),
        in_specs=[pl.BlockSpec(memory_space=pltpu.HBM)] * 2 + [smem] * 2,
        out_specs=vmem,
        scratch_shapes=[
            pltpu.VMEM((CHUNKS, NB, BLK, FEAT), jnp.bfloat16),
            pltpu.VMEM((CHUNKS, 2, CHIPS, NB, ROWS, HALF), jnp.bfloat16),
            pltpu.VMEM((CHUNKS, SPLIT, REPL, SLOTS, ROWS, HALF), jnp.bfloat16),
            pltpu.VMEM((4, CHUNKS, SPLIT, 2, CHIPS, SLOTS, ROWS, HALF), jnp.bfloat16),
            pltpu.VMEM((D, COLS), jnp.bfloat16),
            pltpu.VMEM((rows, COLS), jnp.float32),
            pltpu.VMEM((rows, HB), jnp.float32),
            pltpu.VMEM((SPLIT, CHIPS, SLOTS, ROWS, HD), jnp.float32),
            pltpu.VMEM((SPLIT, CHIPS, SLOTS, ROWS, HD), jnp.float32),
            pltpu.SemaphoreType.DMA((CHUNKS,)),
            pltpu.SemaphoreType.DMA,
            pltpu.SemaphoreType.DMA((CHUNKS,)),
            pltpu.SemaphoreType.DMA((CHUNKS,)),
            pltpu.SemaphoreType.DMA((CHUNKS, SPLIT)),
            pltpu.SemaphoreType.DMA((CHUNKS, SPLIT)),
            pltpu.SemaphoreType.DMA((6, CHUNKS, SPLIT)),
            pltpu.SemaphoreType.DMA((6, CHUNKS, SPLIT)),
        ] + [pltpu.VMEM((REPL, NB, ROWS, HALF), jnp.bfloat16)] * CHUNKS,
        compiler_params=pltpu.CompilerParams(
            collective_id=0, has_side_effects=True, vmem_limit_bytes=VMEM_BYTES),
        cost_estimate=pl.CostEstimate(
            flops=2 * rows * D * COLS, bytes_accessed=D * COLS * 2 + rows * COLS * 4, transcendentals=0),
    )(acts[0, :, 0], w_qkv[0], by_document, block_source)
    return attention(qkv, by_document, block_source)[None]


def solution(mesh):
    placed = (P("section", None, "dp", None, "tensor"), P("section", None, "tensor"), P(), P())
    return jax.shard_map(
        functools.partial(local, mesh.shape["section"], mesh.shape["tensor"]),
        mesh=mesh, in_specs=placed, out_specs=P("section", "dp", "tensor"), check_vma=False,
    )
```

```python
import functools
import math

import jax
import jax.numpy as jnp
from jax import lax
from jax.experimental import pallas as pl
from jax.experimental.pallas import tpu as pltpu
from jax.sharding import PartitionSpec as P

HD = 128
HB = 128
BLK = 128
DOCS = 4
TOK_DEV = 512
GQ = 8
NB = 4
D = 4096
LOCAL = 1024
COLS = 1280
CHIPS = 8
REPL = 16
CHUNKS = 4
FEAT = LOCAL // CHUNKS
HALF = FEAT // 2
ROWS = 16
AHEAD = 2
EARLY = 1
SPLIT = 1
SLOTS = NB // SPLIT
VMEM_BYTES = 60 * 1024 * 1024
GROUP = 8

norm_eps = 1e-05
rope_theta = 500000.0
MESH = pl.DeviceIdType.MESH


def far_first(step, chip, core):
    size = lax.div(step + 1, 2)
    odd = lax.rem(step, 2)
    offset = (1 - odd) * (CHIPS // 2 - size) - odd * lax.rem(size, CHIPS // 2)
    return lax.rem(chip + CHIPS + (1 - 2 * core) * offset, CHIPS)


def near_first(step, chip, core):
    size = lax.div(step + 1, 2)
    offset = (2 * lax.rem(step, 2) - 1) * size
    return lax.rem(chip + CHIPS + (1 - 2 * core) * offset, CHIPS)


def slot_docs(bs_ref, len_ref, section, block, offset_iota):
    window = block // NB
    offset = (block % NB) * BLK + offset_iota
    end = len_ref[section, 0, window]
    start = jnp.zeros_like(offset)
    document = jnp.zeros_like(offset)
    for d in range(DOCS):
        past = offset >= end
        document = document + past.astype(jnp.int32)
        start = jnp.where(past, end, start)
        if d < DOCS - 1:
            end = end + len_ref[section, d + 1, window]
    return window * DOCS + document, offset - start


def exchange_kernel(
    sections, tensors, acts_ref, w_ref, len_ref, bs_ref, qkv_ref,
    rows_in, sbuf, obuf, x, wv, acc, squares, cos_t, sin_t,
    a_sem, w_sem, p1_send, p1_recv, p2_send, p2_recv, y_send, y_recv, *mid
):
    s = lax.axis_index("section")
    i = lax.axis_index("dp")
    t = lax.axis_index("tensor")
    chip, core = i // 2, i % 2
    s_next = (s + 1) % sections
    s_prev = (s + sections - 1) % sections
    t_right = (t + 1) % tensors
    t_left = (t + tensors - 1) % tensors
    t_far = (t + 2) % tensors

    def fetch(c):
        return pltpu.make_async_copy(
            acts_ref.at[:, :, pl.ds(c * FEAT, FEAT)], rows_in.at[c], a_sem.at[c])

    for c in range(CHUNKS):
        fetch(c).start()
    w_copy = pltpu.make_async_copy(w_ref, wv, w_sem)
    w_copy.start()

    barrier = pltpu.get_barrier_semaphore()

    def greet(q, carry):
        pl.semaphore_signal(barrier, inc=1, device_id=(s_prev, q, t), device_id_type=MESH)
        return carry

    def greet_peer(q, carry):
        peer = (i + q) % REPL
        pl.semaphore_signal(barrier, inc=1, device_id=(s, peer, t), device_id_type=MESH)
        return carry

    lax.fori_loop(0, REPL, greet, 0)
    lax.fori_loop(1, REPL, greet_peer, 0)
    pl.semaphore_signal(barrier, inc=1, device_id=(s, i, t_right), device_id_type=MESH)
    pl.semaphore_signal(barrier, inc=1, device_id=(s, i, t_left), device_id_type=MESH)

    row_id = lax.broadcasted_iota(jnp.int32, (2 * HB, 2 * HB), 0)
    col_id = lax.broadcasted_iota(jnp.int32, (2 * HB, 2 * HB), 1)
    shared = row_id & col_id & (HB - 1)
    shared = shared ^ (shared >> 4)
    shared = shared ^ (shared >> 2)
    shared = shared ^ (shared >> 1)
    sign = (1 - 2 * (shared & 1)).astype(jnp.float32)
    signs = jnp.where((row_id // HB) == (col_id // HB), sign, 0.0).astype(jnp.bfloat16)

    def rotate(c):
        fetch(c).wait()
        for part in range(FEAT // (2 * HB)):
            first = part * 2 * HB
            block_rows = rows_in[c, :, :, first:first + 2 * HB].reshape(NB * BLK, 2 * HB)
            turned = jnp.dot(block_rows, signs, preferred_element_type=jnp.float32)
            low = (turned * (1.0 / math.sqrt(HB))).astype(jnp.bfloat16)
            for piece in range(2):
                column = part * 2 * HB + piece * HB
                h, inside = column // HALF, column % HALF
                values = low[:, piece * HB:(piece + 1) * HB].reshape(NB, CHIPS, ROWS, HB)
                for l in range(NB):
                    sbuf[c, h, :, l, :, inside:inside + HB] = values[l]

    def spread(c):
        def send(e, carry):
            to_chip = far_first(lax.rem(e, CHIPS), chip, core)
            to_core = lax.rem(lax.div(e, CHIPS) + 1 + core, 2)
            pltpu.make_async_remote_copy(
                src_ref=sbuf.at[c, to_core, to_chip],
                dst_ref=mid[c].at[i],
                send_sem=p1_send.at[c],
                recv_sem=p1_recv.at[c],
                device_id=(s_next, to_chip * 2 + to_core, t),
                device_id_type=MESH,
            ).start()
            return carry

        lax.fori_loop(0, REPL, send, 0)

    def pick(c, j, k):
        block = bs_ref[s, j * NB + k]
        return mid[c][lax.rem(block, REPL), lax.div(block, REPL)]

    def deliver(c):
        pltpu.make_async_copy(mid[c], mid[c], p1_recv.at[c]).wait()

        for part in range(SPLIT):
            slots = range(part * SLOTS, (part + 1) * SLOTS)

            def choose(j, carry):
                for k in slots:
                    obuf[c, part, j, k % SLOTS] = pick(c, j, k)
                return carry

            def send(e, carry):
                to_chip = near_first(lax.div(e, 2), chip, core)
                to_core = lax.rem(e + core, 2)
                j = to_chip * 2 + to_core
                pltpu.make_async_remote_copy(
                    src_ref=obuf.at[c, part, j],
                    dst_ref=x.at[t, c, part, core, chip],
                    send_sem=p2_send.at[c, part],
                    recv_sem=p2_recv.at[c, part],
                    device_id=(s, j, t),
                    device_id_type=MESH,
                ).start()
                return carry

            lax.fori_loop(0, REPL, choose, 0)
            lax.fori_loop(1, REPL, send, 0)
            for k in slots:
                x[t, c, part, core, chip, k % SLOTS] = pick(c, i, k)

    def delivered(c, part, sem):
        view = obuf.at[c, part, pl.ds(0, REPL - 1)]
        return pltpu.make_async_copy(view, view, sem.at[c, part])

    def y_copy(way, c, part):
        to_left, turn = way % 2, way // 2
        owner = t if turn < 2 else (t_right if to_left else t_left)
        half = (turn + to_left) % 2
        view = x.at[owner, c, part, half]
        return pltpu.make_async_remote_copy(
            src_ref=view, dst_ref=view, send_sem=y_send.at[way, c, part], recv_sem=y_recv.at[way, c, part],
            device_id=(s, i, t_left if to_left else t_right), device_id_type=MESH)

    def gather_start(c, part):
        delivered(c, part, p2_recv).wait()
        for way in range(4):
            y_copy(way, c, part).start()

    def gather_forward(c, part):
        for way in range(2):
            y_copy(way, c, part).wait_recv()
            y_copy(way + 4, c, part).start()

    def gather_near(c, part):
        for way in range(2, 4):
            y_copy(way, c, part).wait_recv()

    def gather_far(c, part):
        for way in range(4, 6):
            y_copy(way, c, part).wait_recv()

    def piece(u, c, part):
        halves = [x[u, c, part, h].reshape(SLOTS * BLK, HALF) for h in range(2)]
        return jnp.concatenate(halves, axis=1)

    def multiply(c, part, owners):
        rows = pl.ds(part * SLOTS * BLK, SLOTS * BLK)
        pieces = [piece(u, c, part) for u in owners]
        for value in pieces:
            wide = value.astype(jnp.float32)
            wide = wide * wide
            total = wide[:, :HB]
            for g in range(1, FEAT // HB):
                total = total + wide[:, g * HB:(g + 1) * HB]
            squares[rows] += total

        def tile(n, carry):
            columns = pl.ds(pl.multiple_of(n * 256, 256), 256)
            result = acc[rows, columns]
            for u, value in zip(owners, pieces):
                rows_w = pl.ds(pl.multiple_of(u * LOCAL + c * FEAT, FEAT), FEAT)
                result = result + jnp.dot(value, wv[rows_w, columns], preferred_element_type=jnp.float32)
            acc[rows, columns] = result
            return carry

        lax.fori_loop(0, COLS // 256, tile, 0)

    def project(c, part):
        gather_near(c, part)
        gather_far(c, part)
        multiply(c, part, [t, t_left, t_right, t_far])

    def finish(part):
        rows = pl.ds(part * SLOTS * BLK, SLOTS * BLK)
        mean = jnp.sum(squares[rows], axis=1, keepdims=True) * (1.0 / D)
        scale = lax.rsqrt(mean + norm_eps)
        cosine = cos_t[part].reshape(SLOTS * BLK, HD) * scale
        sine = sin_t[part].reshape(SLOTS * BLK, HD) * scale

        def put(head, result):
            low = result.astype(jnp.bfloat16).reshape(CHIPS, SLOTS, ROWS, HD)
            for k in range(SLOTS):
                first = (part * SLOTS + k) * BLK
                qkv_ref[first:first + BLK, head * HD:(head + 1) * HD] = low[:, k].reshape(BLK, HD)

        for head in range(GQ + 1):
            values = acc[rows, head * HD:(head + 1) * HD]
            swapped = pltpu.roll(values, HD // 2, 1)
            put(head, values * cosine + swapped * sine)
        last = (GQ + 1) * HD
        put(GQ + 1, acc[rows, last:last + HD] * scale)

    rotate(0)
    pl.semaphore_wait(barrier, 2 * REPL + 1)
    spread(0)
    for c in range(1, CHUNKS):
        rotate(c)
        if c < AHEAD:
            spread(c)

    acc[...] = jnp.zeros_like(acc)
    squares[...] = jnp.zeros_like(squares)
    lane = lax.broadcasted_iota(jnp.int32, (BLK, HD), 1)
    row = lax.broadcasted_iota(jnp.int32, (BLK, HD), 0)
    steps_f = (lane % (HD // 2)).astype(jnp.float32)
    inv_freq = jnp.exp(-math.log(rope_theta) * 2.0 * steps_f / HD)
    for k in range(NB):
        block = bs_ref[s, i * NB + k]
        _, position = slot_docs(bs_ref, len_ref, s, block, row)
        angles = position.astype(jnp.float32) * inv_freq
        sine = jnp.sin(angles)
        sine = jnp.where(lane < HD // 2, -sine, sine)
        cos_t[k // SLOTS, :, k % SLOTS] = jnp.cos(angles).reshape(CHIPS, ROWS, HD)
        sin_t[k // SLOTS, :, k % SLOTS] = sine.reshape(CHIPS, ROWS, HD)

    w_copy.wait()
    for c in range(AHEAD):
        deliver(c)
        spread(c + AHEAD)
    waiting = []
    for c in range(CHUNKS):
        for part in range(SPLIT):
            gather_start(c, part)
            if c >= CHUNKS - AHEAD and len(waiting) > 1:
                project(*waiting.pop(0))
            gather_forward(c, part)
            waiting.append((c, part))
        if c + AHEAD < CHUNKS:
            deliver(c + AHEAD)
            while len(waiting) > EARLY:
                project(*waiting.pop(0))
    while len(waiting) > 1:
        project(*waiting.pop(0))
    for part in range(SPLIT - 1):
        finish(part)
    c, part = waiting[0]
    gather_near(c, part)
    multiply(c, part, [t, t_left, t_right])
    gather_far(c, part)
    multiply(c, part, [t_far])
    finish(part)

    for c in range(CHUNKS):
        pltpu.make_async_copy(sbuf.at[c], sbuf.at[c], p1_send.at[c]).wait()
        for part in range(SPLIT):
            delivered(c, part, p2_send).wait()
            for way in range(6):
                y_copy(way, c, part).wait_send()


def attention_kernel(qkv_in, len_ref, bs_ref, out_ref, qkv_ref, keys, values, context, in_sem, out_sem):
    fetch = pltpu.make_async_copy(qkv_in, qkv_ref, in_sem)
    fetch.start()
    s = lax.axis_index("section")
    i = lax.axis_index("dp")
    blocks = [bs_ref[s, i * NB + k] for k in range(NB)]
    ranks = [sum((other < block).astype(jnp.int32) for other in blocks) for block in blocks]
    slots = [sum(k * (ranks[k] == r).astype(jnp.int32) for k in range(NB)) for r in range(NB)]
    ordered = [sum(blocks[k] * (ranks[k] == r).astype(jnp.int32) for k in range(NB)) for r in range(NB)]
    across = lax.broadcasted_iota(jnp.int32, (1, BLK), 1)
    down = lax.broadcasted_iota(jnp.int32, (BLK, 1), 0)
    key_docs = [slot_docs(bs_ref, len_ref, s, block, across) for block in ordered]
    slot_rows = [pl.ds(pl.multiple_of(slot * BLK, BLK), BLK) for slot in slots]
    fetch.wait()
    for r in range(NB):
        keys[:, r * BLK:(r + 1) * BLK] = qkv_ref[slot_rows[r], GQ * HD:(GQ + 1) * HD].T
        values[r * BLK:(r + 1) * BLK] = qkv_ref[slot_rows[r], (GQ + 1) * HD:]
    factor = math.log2(math.e) / math.sqrt(HD)

    def attend(r, first):
        row_doc, row_pos = slot_docs(bs_ref, len_ref, s, ordered[r], down)
        key_doc = jnp.concatenate([key_docs[f][0] for f in range(first, r + 1)], axis=1)
        key_pos = jnp.concatenate([key_docs[f][1] for f in range(first, r + 1)], axis=1)
        seen = (row_doc == key_doc) & (key_pos <= row_pos)
        near = slice(first * BLK, (r + 1) * BLK)
        near_keys, near_values = keys[:, near], values[near]
        for head in range(0, GQ, GROUP):
            group = range(head, head + GROUP)
            scores = [
                jnp.dot(qkv_ref[slot_rows[r], h * HD:(h + 1) * HD], near_keys, preferred_element_type=jnp.float32)
                for h in group
            ]
            scores = [jnp.where(seen, value, -1e30) for value in scores]
            row_max = [jnp.max(value, axis=1, keepdims=True) for value in scores]
            probs = [jnp.exp2((value - top) * factor) for value, top in zip(scores, row_max)]
            totals = [jnp.sum(value, axis=1, keepdims=True) for value in probs]
            sums = [
                jnp.dot(value.astype(jnp.bfloat16), near_values, preferred_element_type=jnp.float32)
                for value in probs
            ]
            for h, value, total in zip(group, sums, totals):
                context[r, :, h * HD:(h + 1) * HD] = (value / total).astype(jnp.bfloat16)

    copies = []
    for r in range(NB):
        same = [(ordered[f] // NB == ordered[r] // NB).astype(jnp.int32) for f in range(r)]
        count = sum(same) if same else jnp.int32(0)
        for earlier in range(r + 1):
            pl.when(count == earlier)(functools.partial(attend, r, r - earlier))
        copies.append(pltpu.make_async_copy(context.at[r], out_ref.at[slot_rows[r]], out_sem.at[r]))
        copies[r].start()
    for copy in copies:
        copy.wait()


def attention(qkv, by_document, block_source):
    rows = NB * BLK
    vmem = pl.BlockSpec(memory_space=pltpu.VMEM)
    smem = pl.BlockSpec(memory_space=pltpu.SMEM)
    return pl.pallas_call(
        attention_kernel,
        out_shape=jax.ShapeDtypeStruct((rows, GQ * HD), jnp.bfloat16),
        in_specs=[pl.BlockSpec(memory_space=pltpu.HBM), smem, smem],
        out_specs=pl.BlockSpec(memory_space=pl.ANY),
        scratch_shapes=[
            pltpu.VMEM((rows, COLS), jnp.bfloat16),
            pltpu.VMEM((HD, rows), jnp.bfloat16),
            pltpu.VMEM((rows, HD), jnp.bfloat16),
            pltpu.VMEM((NB, BLK, GQ * HD), jnp.bfloat16),
            pltpu.SemaphoreType.DMA,
            pltpu.SemaphoreType.DMA((NB,)),
        ],
        compiler_params=pltpu.CompilerParams(vmem_limit_bytes=VMEM_BYTES),
        cost_estimate=pl.CostEstimate(
            flops=4 * GQ * rows * rows * HD, bytes_accessed=rows * COLS * 4, transcendentals=GQ * rows * rows),
    )(qkv, by_document, block_source)


def local(sections, tensors, acts, w_qkv, lengths, block_source):
    rows = NB * BLK
    by_document = lengths.transpose(0, 2, 1)
    vmem = pl.BlockSpec(memory_space=pltpu.VMEM)
    smem = pl.BlockSpec(memory_space=pltpu.SMEM)
    qkv = pl.pallas_call(
        functools.partial(exchange_kernel, sections, tensors),
        out_shape=jax.ShapeDtypeStruct((rows, COLS), jnp.bfloat16),
        in_specs=[pl.BlockSpec(memory_space=pltpu.HBM)] * 2 + [smem] * 2,
        out_specs=vmem,
        scratch_shapes=[
            pltpu.VMEM((CHUNKS, NB, BLK, FEAT), jnp.bfloat16),
            pltpu.VMEM((CHUNKS, 2, CHIPS, NB, ROWS, HALF), jnp.bfloat16),
            pltpu.VMEM((CHUNKS, SPLIT, REPL, SLOTS, ROWS, HALF), jnp.bfloat16),
            pltpu.VMEM((4, CHUNKS, SPLIT, 2, CHIPS, SLOTS, ROWS, HALF), jnp.bfloat16),
            pltpu.VMEM((D, COLS), jnp.bfloat16),
            pltpu.VMEM((rows, COLS), jnp.float32),
            pltpu.VMEM((rows, HB), jnp.float32),
            pltpu.VMEM((SPLIT, CHIPS, SLOTS, ROWS, HD), jnp.float32),
            pltpu.VMEM((SPLIT, CHIPS, SLOTS, ROWS, HD), jnp.float32),
            pltpu.SemaphoreType.DMA((CHUNKS,)),
            pltpu.SemaphoreType.DMA,
            pltpu.SemaphoreType.DMA((CHUNKS,)),
            pltpu.SemaphoreType.DMA((CHUNKS,)),
            pltpu.SemaphoreType.DMA((CHUNKS, SPLIT)),
            pltpu.SemaphoreType.DMA((CHUNKS, SPLIT)),
            pltpu.SemaphoreType.DMA((6, CHUNKS, SPLIT)),
            pltpu.SemaphoreType.DMA((6, CHUNKS, SPLIT)),
        ] + [pltpu.VMEM((REPL, NB, ROWS, HALF), jnp.bfloat16)] * CHUNKS,
        compiler_params=pltpu.CompilerParams(
            collective_id=0, has_side_effects=True, vmem_limit_bytes=VMEM_BYTES),
        cost_estimate=pl.CostEstimate(
            flops=2 * rows * D * COLS, bytes_accessed=D * COLS * 2 + rows * COLS * 4, transcendentals=0),
    )(acts[0, :, 0], w_qkv[0], by_document, block_source)
    return attention(qkv, by_document, block_source)[None]


def solution(mesh):
    placed = (P("section", None, "dp", None, "tensor"), P("section", None, "tensor"), P(), P())
    return jax.shard_map(
        functools.partial(local, mesh.shape["section"], mesh.shape["tensor"]),
        mesh=mesh, in_specs=placed, out_specs=P("section", "dp", "tensor"), check_vma=False,
    )
```

```python
import functools
import math

import jax
import jax.numpy as jnp
from jax import lax
from jax.experimental import pallas as pl
from jax.experimental.pallas import tpu as pltpu
from jax.sharding import PartitionSpec as P

HD = 128
HB = 128
BLK = 128
DOCS = 4
TOK_DEV = 512
GQ = 8
NB = 4
D = 4096
LOCAL = 1024
COLS = 1280
CHIPS = 8
REPL = 16
CHUNKS = 4
FEAT = LOCAL // CHUNKS
HALF = FEAT // 2
ROWS = 16
AHEAD = 2
EARLY = 1
SPLIT = 1
SLOTS = NB // SPLIT
VMEM_BYTES = 48 * 1024 * 1024
GROUP = 8

norm_eps = 1e-05
rope_theta = 500000.0
MESH = pl.DeviceIdType.MESH


def far_first(step, chip, core):
    size = lax.div(step + 1, 2)
    odd = lax.rem(step, 2)
    offset = (1 - odd) * (CHIPS // 2 - size) - odd * lax.rem(size, CHIPS // 2)
    return lax.rem(chip + CHIPS + (1 - 2 * core) * offset, CHIPS)


def near_first(step, chip, core):
    size = lax.div(step + 1, 2)
    offset = (2 * lax.rem(step, 2) - 1) * size
    return lax.rem(chip + CHIPS + (1 - 2 * core) * offset, CHIPS)


def slot_docs(bs_ref, len_ref, section, block, offset_iota):
    window = block // NB
    offset = (block % NB) * BLK + offset_iota
    end = len_ref[section, 0, window]
    start = jnp.zeros_like(offset)
    document = jnp.zeros_like(offset)
    for d in range(DOCS):
        past = offset >= end
        document = document + past.astype(jnp.int32)
        start = jnp.where(past, end, start)
        if d < DOCS - 1:
            end = end + len_ref[section, d + 1, window]
    return window * DOCS + document, offset - start


def exchange_kernel(
    sections, tensors, acts_ref, w_ref, len_ref, bs_ref, qkv_ref,
    sbuf, obuf, x, wv, acc, squares, cos_t, sin_t,
    w_sem, p1_send, p1_recv, p2_send, p2_recv, y_send, y_recv, *mid
):
    s = lax.axis_index("section")
    i = lax.axis_index("dp")
    t = lax.axis_index("tensor")
    chip, core = i // 2, i % 2
    s_next = (s + 1) % sections
    s_prev = (s + sections - 1) % sections
    t_right = (t + 1) % tensors
    t_left = (t + tensors - 1) % tensors
    t_far = (t + 2) % tensors

    w_copy = pltpu.make_async_copy(w_ref, wv, w_sem)
    w_copy.start()

    barrier = pltpu.get_barrier_semaphore()

    def greet(q, carry):
        pl.semaphore_signal(barrier, inc=1, device_id=(s_prev, q, t), device_id_type=MESH)
        return carry

    def greet_peer(q, carry):
        peer = (i + q) % REPL
        pl.semaphore_signal(barrier, inc=1, device_id=(s, peer, t), device_id_type=MESH)
        return carry

    lax.fori_loop(0, REPL, greet, 0)
    lax.fori_loop(1, REPL, greet_peer, 0)
    pl.semaphore_signal(barrier, inc=1, device_id=(s, i, t_right), device_id_type=MESH)
    pl.semaphore_signal(barrier, inc=1, device_id=(s, i, t_left), device_id_type=MESH)

    row_id = lax.broadcasted_iota(jnp.int32, (2 * HB, 2 * HB), 0)
    col_id = lax.broadcasted_iota(jnp.int32, (2 * HB, 2 * HB), 1)
    shared = row_id & col_id & (HB - 1)
    shared = shared ^ (shared >> 4)
    shared = shared ^ (shared >> 2)
    shared = shared ^ (shared >> 1)
    sign = (1 - 2 * (shared & 1)).astype(jnp.float32)
    signs = jnp.where((row_id // HB) == (col_id // HB), sign, 0.0).astype(jnp.bfloat16)

    def rotate(c):
        for part in range(FEAT // (2 * HB)):
            first = c * FEAT + part * 2 * HB
            block_rows = acts_ref[:, :, first:first + 2 * HB].reshape(NB * BLK, 2 * HB)
            turned = jnp.dot(block_rows, signs, preferred_element_type=jnp.float32)
            low = (turned * (1.0 / math.sqrt(HB))).astype(jnp.bfloat16)
            for piece in range(2):
                column = part * 2 * HB + piece * HB
                h, inside = column // HALF, column % HALF
                values = low[:, piece * HB:(piece + 1) * HB].reshape(NB, CHIPS, ROWS, HB)
                for l in range(NB):
                    sbuf[c, h, :, l, :, inside:inside + HB] = values[l]

    def spread(c):
        def send(e, carry):
            to_chip = far_first(lax.rem(e, CHIPS), chip, core)
            to_core = lax.rem(lax.div(e, CHIPS) + 1 + core, 2)
            pltpu.make_async_remote_copy(
                src_ref=sbuf.at[c, to_core, to_chip],
                dst_ref=mid[c].at[i],
                send_sem=p1_send.at[c],
                recv_sem=p1_recv.at[c],
                device_id=(s_next, to_chip * 2 + to_core, t),
                device_id_type=MESH,
            ).start()
            return carry

        lax.fori_loop(0, REPL, send, 0)

    def pick(c, j, k):
        block = bs_ref[s, j * NB + k]
        return mid[c][lax.rem(block, REPL), lax.div(block, REPL)]

    def deliver(c):
        pltpu.make_async_copy(mid[c], mid[c], p1_recv.at[c]).wait()

        for part in range(SPLIT):
            slots = range(part * SLOTS, (part + 1) * SLOTS)

            def choose(j, carry):
                for k in slots:
                    obuf[c, part, j, k % SLOTS] = pick(c, j, k)
                return carry

            def send(e, carry):
                to_chip = near_first(lax.div(e, 2), chip, core)
                to_core = lax.rem(e + core, 2)
                j = to_chip * 2 + to_core
                pltpu.make_async_remote_copy(
                    src_ref=obuf.at[c, part, j],
                    dst_ref=x.at[t, c, part, core, chip],
                    send_sem=p2_send.at[c, part],
                    recv_sem=p2_recv.at[c, part],
                    device_id=(s, j, t),
                    device_id_type=MESH,
                ).start()
                return carry

            lax.fori_loop(0, REPL, choose, 0)
            lax.fori_loop(1, REPL, send, 0)
            for k in slots:
                x[t, c, part, core, chip, k % SLOTS] = pick(c, i, k)

    def delivered(c, part, sem):
        view = obuf.at[c, part, pl.ds(0, REPL - 1)]
        return pltpu.make_async_copy(view, view, sem.at[c, part])

    def y_copy(way, c, part):
        to_left, turn = way % 2, way // 2
        owner = t if turn < 2 else (t_right if to_left else t_left)
        half = (turn + to_left) % 2
        view = x.at[owner, c, part, half]
        return pltpu.make_async_remote_copy(
            src_ref=view, dst_ref=view, send_sem=y_send.at[way, c, part], recv_sem=y_recv.at[way, c, part],
            device_id=(s, i, t_left if to_left else t_right), device_id_type=MESH)

    def gather_start(c, part):
        delivered(c, part, p2_recv).wait()
        for way in range(4):
            y_copy(way, c, part).start()

    def gather_forward(c, part):
        for way in range(2):
            y_copy(way, c, part).wait_recv()
            y_copy(way + 4, c, part).start()

    def gather_near(c, part):
        for way in range(2, 4):
            y_copy(way, c, part).wait_recv()

    def gather_far(c, part):
        for way in range(4, 6):
            y_copy(way, c, part).wait_recv()

    def piece(u, c, part):
        halves = [x[u, c, part, h].reshape(SLOTS * BLK, HALF) for h in range(2)]
        return jnp.concatenate(halves, axis=1)

    def multiply(c, part, owners):
        rows = pl.ds(part * SLOTS * BLK, SLOTS * BLK)
        pieces = [piece(u, c, part) for u in owners]
        for value in pieces:
            wide = value.astype(jnp.float32)
            wide = wide * wide
            total = wide[:, :HB]
            for g in range(1, FEAT // HB):
                total = total + wide[:, g * HB:(g + 1) * HB]
            squares[rows] += total

        def tile(n, carry):
            columns = pl.ds(pl.multiple_of(n * 256, 256), 256)
            result = acc[rows, columns]
            for u, value in zip(owners, pieces):
                rows_w = pl.ds(pl.multiple_of(u * LOCAL + c * FEAT, FEAT), FEAT)
                result = result + jnp.dot(value, wv[rows_w, columns], preferred_element_type=jnp.float32)
            acc[rows, columns] = result
            return carry

        lax.fori_loop(0, COLS // 256, tile, 0)

    def project(c, part):
        gather_near(c, part)
        gather_far(c, part)
        multiply(c, part, [t, t_left, t_right, t_far])

    def finish(part):
        rows = pl.ds(part * SLOTS * BLK, SLOTS * BLK)
        mean = jnp.sum(squares[rows], axis=1, keepdims=True) * (1.0 / D)
        scale = lax.rsqrt(mean + norm_eps)
        cosine = cos_t[part].reshape(SLOTS * BLK, HD) * scale
        sine = sin_t[part].reshape(SLOTS * BLK, HD) * scale

        def put(head, result):
            low = result.astype(jnp.bfloat16).reshape(CHIPS, SLOTS, ROWS, HD)
            for k in range(SLOTS):
                first = (part * SLOTS + k) * BLK
                qkv_ref[first:first + BLK, head * HD:(head + 1) * HD] = low[:, k].reshape(BLK, HD)

        for head in range(GQ + 1):
            values = acc[rows, head * HD:(head + 1) * HD]
            swapped = pltpu.roll(values, HD // 2, 1)
            put(head, values * cosine + swapped * sine)
        last = (GQ + 1) * HD
        put(GQ + 1, acc[rows, last:last + HD] * scale)

    rotate(0)
    pl.semaphore_wait(barrier, 2 * REPL + 1)
    spread(0)
    for c in range(1, CHUNKS):
        rotate(c)
        if c < AHEAD:
            spread(c)

    acc[...] = jnp.zeros_like(acc)
    squares[...] = jnp.zeros_like(squares)
    lane = lax.broadcasted_iota(jnp.int32, (BLK, HD), 1)
    row = lax.broadcasted_iota(jnp.int32, (BLK, HD), 0)
    steps_f = (lane % (HD // 2)).astype(jnp.float32)
    inv_freq = jnp.exp(-math.log(rope_theta) * 2.0 * steps_f / HD)
    for k in range(NB):
        block = bs_ref[s, i * NB + k]
        _, position = slot_docs(bs_ref, len_ref, s, block, row)
        angles = position.astype(jnp.float32) * inv_freq
        sine = jnp.sin(angles)
        sine = jnp.where(lane < HD // 2, -sine, sine)
        cos_t[k // SLOTS, :, k % SLOTS] = jnp.cos(angles).reshape(CHIPS, ROWS, HD)
        sin_t[k // SLOTS, :, k % SLOTS] = sine.reshape(CHIPS, ROWS, HD)

    w_copy.wait()
    for c in range(AHEAD):
        deliver(c)
        spread(c + AHEAD)
    waiting = []
    for c in range(CHUNKS):
        for part in range(SPLIT):
            gather_start(c, part)
            if c >= CHUNKS - AHEAD and len(waiting) > 1:
                project(*waiting.pop(0))
            gather_forward(c, part)
            waiting.append((c, part))
        if c + AHEAD < CHUNKS:
            deliver(c + AHEAD)
            while len(waiting) > EARLY:
                project(*waiting.pop(0))
    while len(waiting) > 1:
        project(*waiting.pop(0))
    for part in range(SPLIT - 1):
        finish(part)
    c, part = waiting[0]
    gather_near(c, part)
    multiply(c, part, [t, t_left, t_right])
    gather_far(c, part)
    multiply(c, part, [t_far])
    finish(part)

    for c in range(CHUNKS):
        pltpu.make_async_copy(sbuf.at[c], sbuf.at[c], p1_send.at[c]).wait()
        for part in range(SPLIT):
            delivered(c, part, p2_send).wait()
            for way in range(6):
                y_copy(way, c, part).wait_send()


def attention_kernel(qkv_ref, len_ref, bs_ref, out_ref, keys, values, context, out_sem):
    s = lax.axis_index("section")
    i = lax.axis_index("dp")
    blocks = [bs_ref[s, i * NB + k] for k in range(NB)]
    ranks = [sum((other < block).astype(jnp.int32) for other in blocks) for block in blocks]
    slots = [sum(k * (ranks[k] == r).astype(jnp.int32) for k in range(NB)) for r in range(NB)]
    ordered = [sum(blocks[k] * (ranks[k] == r).astype(jnp.int32) for k in range(NB)) for r in range(NB)]
    across = lax.broadcasted_iota(jnp.int32, (1, BLK), 1)
    down = lax.broadcasted_iota(jnp.int32, (BLK, 1), 0)
    key_docs = [slot_docs(bs_ref, len_ref, s, block, across) for block in ordered]
    slot_rows = [pl.ds(pl.multiple_of(slot * BLK, BLK), BLK) for slot in slots]
    for r in range(NB):
        keys[:, r * BLK:(r + 1) * BLK] = qkv_ref[slot_rows[r], GQ * HD:(GQ + 1) * HD].T
        values[r * BLK:(r + 1) * BLK] = qkv_ref[slot_rows[r], (GQ + 1) * HD:]
    factor = math.log2(math.e) / math.sqrt(HD)

    def attend(r, first):
        row_doc, row_pos = slot_docs(bs_ref, len_ref, s, ordered[r], down)
        key_doc = jnp.concatenate([key_docs[f][0] for f in range(first, r + 1)], axis=1)
        key_pos = jnp.concatenate([key_docs[f][1] for f in range(first, r + 1)], axis=1)
        seen = (row_doc == key_doc) & (key_pos <= row_pos)
        near = slice(first * BLK, (r + 1) * BLK)
        near_keys, near_values = keys[:, near], values[near]
        for head in range(0, GQ, GROUP):
            group = range(head, head + GROUP)
            scores = [
                jnp.dot(qkv_ref[slot_rows[r], h * HD:(h + 1) * HD], near_keys, preferred_element_type=jnp.float32)
                for h in group
            ]
            scores = [jnp.where(seen, value, -1e30) for value in scores]
            row_max = [jnp.max(value, axis=1, keepdims=True) for value in scores]
            probs = [jnp.exp2((value - top) * factor) for value, top in zip(scores, row_max)]
            totals = [jnp.sum(value, axis=1, keepdims=True) for value in probs]
            sums = [
                jnp.dot(value.astype(jnp.bfloat16), near_values, preferred_element_type=jnp.float32)
                for value in probs
            ]
            for h, value, total in zip(group, sums, totals):
                context[r, :, h * HD:(h + 1) * HD] = (value / total).astype(jnp.bfloat16)

    copies = []
    for r in range(NB):
        same = [(ordered[f] // NB == ordered[r] // NB).astype(jnp.int32) for f in range(r)]
        count = sum(same) if same else jnp.int32(0)
        for earlier in range(r + 1):
            pl.when(count == earlier)(functools.partial(attend, r, r - earlier))
        copies.append(pltpu.make_async_copy(context.at[r], out_ref.at[slot_rows[r]], out_sem.at[r]))
        copies[r].start()
    for copy in copies:
        copy.wait()


def attention(qkv, by_document, block_source):
    rows = NB * BLK
    vmem = pl.BlockSpec(memory_space=pltpu.VMEM)
    smem = pl.BlockSpec(memory_space=pltpu.SMEM)
    return pl.pallas_call(
        attention_kernel,
        out_shape=jax.ShapeDtypeStruct((rows, GQ * HD), jnp.bfloat16),
        in_specs=[vmem, smem, smem],
        out_specs=pl.BlockSpec(memory_space=pl.ANY),
        scratch_shapes=[
            pltpu.VMEM((HD, rows), jnp.bfloat16),
            pltpu.VMEM((rows, HD), jnp.bfloat16),
            pltpu.VMEM((NB, BLK, GQ * HD), jnp.bfloat16),
            pltpu.SemaphoreType.DMA((NB,)),
        ],
        compiler_params=pltpu.CompilerParams(vmem_limit_bytes=32 * 1024 * 1024),
        cost_estimate=pl.CostEstimate(
            flops=4 * GQ * rows * rows * HD, bytes_accessed=rows * COLS * 4, transcendentals=GQ * rows * rows),
    )(qkv, by_document, block_source)


def local(sections, tensors, acts, w_qkv, lengths, block_source):
    rows = NB * BLK
    by_document = lengths.transpose(0, 2, 1)
    vmem = pl.BlockSpec(memory_space=pltpu.VMEM)
    smem = pl.BlockSpec(memory_space=pltpu.SMEM)
    qkv = pl.pallas_call(
        functools.partial(exchange_kernel, sections, tensors),
        out_shape=jax.ShapeDtypeStruct((rows, COLS), jnp.bfloat16),
        in_specs=[vmem, pl.BlockSpec(memory_space=pltpu.HBM), smem, smem],
        out_specs=vmem,
        scratch_shapes=[
            pltpu.VMEM((CHUNKS, 2, CHIPS, NB, ROWS, HALF), jnp.bfloat16),
            pltpu.VMEM((CHUNKS, SPLIT, REPL, SLOTS, ROWS, HALF), jnp.bfloat16),
            pltpu.VMEM((4, CHUNKS, SPLIT, 2, CHIPS, SLOTS, ROWS, HALF), jnp.bfloat16),
            pltpu.VMEM((D, COLS), jnp.bfloat16),
            pltpu.VMEM((rows, COLS), jnp.float32),
            pltpu.VMEM((rows, HB), jnp.float32),
            pltpu.VMEM((SPLIT, CHIPS, SLOTS, ROWS, HD), jnp.float32),
            pltpu.VMEM((SPLIT, CHIPS, SLOTS, ROWS, HD), jnp.float32),
            pltpu.SemaphoreType.DMA,
            pltpu.SemaphoreType.DMA((CHUNKS,)),
            pltpu.SemaphoreType.DMA((CHUNKS,)),
            pltpu.SemaphoreType.DMA((CHUNKS, SPLIT)),
            pltpu.SemaphoreType.DMA((CHUNKS, SPLIT)),
            pltpu.SemaphoreType.DMA((6, CHUNKS, SPLIT)),
            pltpu.SemaphoreType.DMA((6, CHUNKS, SPLIT)),
        ] + [pltpu.VMEM((REPL, NB, ROWS, HALF), jnp.bfloat16)] * CHUNKS,
        compiler_params=pltpu.CompilerParams(
            collective_id=0, has_side_effects=True, vmem_limit_bytes=VMEM_BYTES),
        cost_estimate=pl.CostEstimate(
            flops=2 * rows * D * COLS, bytes_accessed=D * COLS * 2 + rows * COLS * 4, transcendentals=0),
    )(acts[0, :, 0], w_qkv[0], by_document, block_source)
    return attention(qkv, by_document, block_source)[None]


def solution(mesh):
    placed = (P("section", None, "dp", None, "tensor"), P("section", None, "tensor"), P(), P())
    return jax.shard_map(
        functools.partial(local, mesh.shape["section"], mesh.shape["tensor"]),
        mesh=mesh, in_specs=placed, out_specs=P("section", "dp", "tensor"), check_vma=False,
    )
```

```python
import functools
import math

import jax
import jax.numpy as jnp
from jax import lax
from jax.experimental import pallas as pl
from jax.experimental.pallas import tpu as pltpu
from jax.sharding import PartitionSpec as P

HD = 128
HB = 128
BLK = 128
DOCS = 4
TOK_DEV = 512
GQ = 8
NB = 4
D = 4096
LOCAL = 1024
COLS = 1280
CHIPS = 8
REPL = 16
CHUNKS = 4
FEAT = LOCAL // CHUNKS
HALF = FEAT // 2
ROWS = 16
AHEAD = 2
EARLY = 1
SPLIT = 1
SLOTS = NB // SPLIT
VMEM_BYTES = 48 * 1024 * 1024
GROUP = 8

norm_eps = 1e-05
rope_theta = 500000.0
MESH = pl.DeviceIdType.MESH


def far_first(step, chip, core):
    size = lax.div(step + 1, 2)
    odd = lax.rem(step, 2)
    offset = (1 - odd) * (CHIPS // 2 - size) - odd * lax.rem(size, CHIPS // 2)
    return lax.rem(chip + CHIPS + (1 - 2 * core) * offset, CHIPS)


def near_first(step, chip, core):
    size = lax.div(step + 1, 2)
    offset = (2 * lax.rem(step, 2) - 1) * size
    return lax.rem(chip + CHIPS + (1 - 2 * core) * offset, CHIPS)


def slot_docs(bs_ref, len_ref, section, block, offset_iota):
    window = block // NB
    offset = (block % NB) * BLK + offset_iota
    end = len_ref[section, 0, window]
    start = jnp.zeros_like(offset)
    document = jnp.zeros_like(offset)
    for d in range(DOCS):
        past = offset >= end
        document = document + past.astype(jnp.int32)
        start = jnp.where(past, end, start)
        if d < DOCS - 1:
            end = end + len_ref[section, d + 1, window]
    return window * DOCS + document, offset - start


def exchange_kernel(
    sections, tensors, acts_ref, w_ref, len_ref, bs_ref, qkv_ref,
    rows_in, sbuf, obuf, x, wv, acc, squares, cos_t, sin_t,
    a_sem, w_sem, p1_send, p1_recv, p2_send, p2_recv, y_send, y_recv, *mid
):
    s = lax.axis_index("section")
    i = lax.axis_index("dp")
    t = lax.axis_index("tensor")
    chip, core = i // 2, i % 2
    s_next = (s + 1) % sections
    s_prev = (s + sections - 1) % sections
    t_right = (t + 1) % tensors
    t_left = (t + tensors - 1) % tensors
    t_far = (t + 2) % tensors

    def fetch(c):
        return pltpu.make_async_copy(
            acts_ref.at[:, :, pl.ds(c * FEAT, FEAT)], rows_in.at[c], a_sem.at[c])

    for c in range(CHUNKS):
        fetch(c).start()
    w_copy = pltpu.make_async_copy(w_ref, wv, w_sem)
    w_copy.start()

    barrier = pltpu.get_barrier_semaphore()

    def greet(q, carry):
        pl.semaphore_signal(barrier, inc=1, device_id=(s_prev, q, t), device_id_type=MESH)
        return carry

    def greet_peer(q, carry):
        peer = (i + q) % REPL
        pl.semaphore_signal(barrier, inc=1, device_id=(s, peer, t), device_id_type=MESH)
        return carry

    lax.fori_loop(0, REPL, greet, 0)
    lax.fori_loop(1, REPL, greet_peer, 0)
    pl.semaphore_signal(barrier, inc=1, device_id=(s, i, t_right), device_id_type=MESH)
    pl.semaphore_signal(barrier, inc=1, device_id=(s, i, t_left), device_id_type=MESH)

    row_id = lax.broadcasted_iota(jnp.int32, (2 * HB, 2 * HB), 0)
    col_id = lax.broadcasted_iota(jnp.int32, (2 * HB, 2 * HB), 1)
    shared = row_id & col_id & (HB - 1)
    shared = shared ^ (shared >> 4)
    shared = shared ^ (shared >> 2)
    shared = shared ^ (shared >> 1)
    sign = (1 - 2 * (shared & 1)).astype(jnp.float32)
    signs = jnp.where((row_id // HB) == (col_id // HB), sign, 0.0).astype(jnp.bfloat16)

    def rotate(c):
        fetch(c).wait()
        for part in range(FEAT // (2 * HB)):
            first = part * 2 * HB
            block_rows = rows_in[c, :, :, first:first + 2 * HB].reshape(NB * BLK, 2 * HB)
            turned = jnp.dot(block_rows, signs, preferred_element_type=jnp.float32)
            low = (turned * (1.0 / math.sqrt(HB))).astype(jnp.bfloat16)
            for piece in range(2):
                column = part * 2 * HB + piece * HB
                h, inside = column // HALF, column % HALF
                values = low[:, piece * HB:(piece + 1) * HB].reshape(NB, CHIPS, ROWS, HB)
                for l in range(NB):
                    sbuf[c, h, :, l, :, inside:inside + HB] = values[l]

    def spread(c):
        def send(e, carry):
            to_chip = far_first(lax.rem(e, CHIPS), chip, core)
            to_core = lax.rem(lax.div(e, CHIPS) + 1 + core, 2)
            pltpu.make_async_remote_copy(
                src_ref=sbuf.at[c, to_core, to_chip],
                dst_ref=mid[c].at[i],
                send_sem=p1_send.at[c],
                recv_sem=p1_recv.at[c],
                device_id=(s_next, to_chip * 2 + to_core, t),
                device_id_type=MESH,
            ).start()
            return carry

        lax.fori_loop(0, REPL, send, 0)

    def pick(c, j, k):
        block = bs_ref[s, j * NB + k]
        return mid[c][lax.rem(block, REPL), lax.div(block, REPL)]

    def deliver(c):
        pltpu.make_async_copy(mid[c], mid[c], p1_recv.at[c]).wait()

        for part in range(SPLIT):
            slots = range(part * SLOTS, (part + 1) * SLOTS)

            def choose(j, carry):
                for k in slots:
                    obuf[c, part, j, k % SLOTS] = pick(c, j, k)
                return carry

            def send(e, carry):
                to_chip = near_first(lax.div(e, 2), chip, core)
                to_core = lax.rem(e + core, 2)
                j = to_chip * 2 + to_core
                pltpu.make_async_remote_copy(
                    src_ref=obuf.at[c, part, j],
                    dst_ref=x.at[t, c, part, core, chip],
                    send_sem=p2_send.at[c, part],
                    recv_sem=p2_recv.at[c, part],
                    device_id=(s, j, t),
                    device_id_type=MESH,
                ).start()
                return carry

            lax.fori_loop(0, REPL, choose, 0)
            lax.fori_loop(1, REPL, send, 0)
            for k in slots:
                x[t, c, part, core, chip, k % SLOTS] = pick(c, i, k)

    def delivered(c, part, sem):
        view = obuf.at[c, part, pl.ds(0, REPL - 1)]
        return pltpu.make_async_copy(view, view, sem.at[c, part])

    def y_copy(way, c, part):
        to_left, turn = way % 2, way // 2
        owner = t if turn < 2 else (t_right if to_left else t_left)
        half = (turn + to_left) % 2
        view = x.at[owner, c, part, half]
        return pltpu.make_async_remote_copy(
            src_ref=view, dst_ref=view, send_sem=y_send.at[way, c, part], recv_sem=y_recv.at[way, c, part],
            device_id=(s, i, t_left if to_left else t_right), device_id_type=MESH)

    def gather_start(c, part):
        delivered(c, part, p2_recv).wait()
        for way in range(4):
            y_copy(way, c, part).start()

    def gather_forward(c, part):
        for way in range(2):
            y_copy(way, c, part).wait_recv()
            y_copy(way + 4, c, part).start()

    def gather_near(c, part):
        for way in range(2, 4):
            y_copy(way, c, part).wait_recv()

    def gather_far(c, part):
        for way in range(4, 6):
            y_copy(way, c, part).wait_recv()

    def piece(u, c, part):
        halves = [x[u, c, part, h].reshape(SLOTS * BLK, HALF) for h in range(2)]
        return jnp.concatenate(halves, axis=1)

    def multiply(c, part, owners):
        rows = pl.ds(part * SLOTS * BLK, SLOTS * BLK)
        pieces = [piece(u, c, part) for u in owners]
        for value in pieces:
            wide = value.astype(jnp.float32)
            wide = wide * wide
            total = wide[:, :HB]
            for g in range(1, FEAT // HB):
                total = total + wide[:, g * HB:(g + 1) * HB]
            squares[rows] += total

        def tile(n, carry):
            columns = pl.ds(pl.multiple_of(n * 256, 256), 256)
            result = acc[rows, columns]
            for u, value in zip(owners, pieces):
                rows_w = pl.ds(pl.multiple_of(u * LOCAL + c * FEAT, FEAT), FEAT)
                result = result + jnp.dot(value, wv[rows_w, columns], preferred_element_type=jnp.float32)
            acc[rows, columns] = result
            return carry

        lax.fori_loop(0, COLS // 256, tile, 0)

    def project(c, part):
        gather_near(c, part)
        gather_far(c, part)
        multiply(c, part, [t, t_left, t_right, t_far])

    def finish(part):
        rows = pl.ds(part * SLOTS * BLK, SLOTS * BLK)
        mean = jnp.sum(squares[rows], axis=1, keepdims=True) * (1.0 / D)
        scale = lax.rsqrt(mean + norm_eps)
        cosine = cos_t[part].reshape(SLOTS * BLK, HD) * scale
        sine = sin_t[part].reshape(SLOTS * BLK, HD) * scale

        def put(head, result):
            low = result.astype(jnp.bfloat16).reshape(CHIPS, SLOTS, ROWS, HD)
            for k in range(SLOTS):
                first = (part * SLOTS + k) * BLK
                qkv_ref[first:first + BLK, head * HD:(head + 1) * HD] = low[:, k].reshape(BLK, HD)

        for head in range(GQ + 1):
            values = acc[rows, head * HD:(head + 1) * HD]
            swapped = pltpu.roll(values, HD // 2, 1)
            put(head, values * cosine + swapped * sine)
        last = (GQ + 1) * HD
        put(GQ + 1, acc[rows, last:last + HD] * scale)

    rotate(0)
    pl.semaphore_wait(barrier, 2 * REPL + 1)
    spread(0)
    for c in range(1, CHUNKS):
        rotate(c)
        if c < AHEAD:
            spread(c)

    acc[...] = jnp.zeros_like(acc)
    squares[...] = jnp.zeros_like(squares)
    lane = lax.broadcasted_iota(jnp.int32, (BLK, HD), 1)
    row = lax.broadcasted_iota(jnp.int32, (BLK, HD), 0)
    steps_f = (lane % (HD // 2)).astype(jnp.float32)
    inv_freq = jnp.exp(-math.log(rope_theta) * 2.0 * steps_f / HD)
    for k in range(NB):
        block = bs_ref[s, i * NB + k]
        _, position = slot_docs(bs_ref, len_ref, s, block, row)
        angles = position.astype(jnp.float32) * inv_freq
        sine = jnp.sin(angles)
        sine = jnp.where(lane < HD // 2, -sine, sine)
        cos_t[k // SLOTS, :, k % SLOTS] = jnp.cos(angles).reshape(CHIPS, ROWS, HD)
        sin_t[k // SLOTS, :, k % SLOTS] = sine.reshape(CHIPS, ROWS, HD)

    w_copy.wait()
    for c in range(AHEAD):
        deliver(c)
        spread(c + AHEAD)
    waiting = []
    for c in range(CHUNKS):
        for part in range(SPLIT):
            gather_start(c, part)
            if c >= CHUNKS - AHEAD and len(waiting) > 1:
                project(*waiting.pop(0))
            gather_forward(c, part)
            waiting.append((c, part))
        if c + AHEAD < CHUNKS:
            deliver(c + AHEAD)
            while len(waiting) > EARLY:
                project(*waiting.pop(0))
    while len(waiting) > 1:
        project(*waiting.pop(0))
    for part in range(SPLIT - 1):
        finish(part)
    c, part = waiting[0]
    gather_near(c, part)
    multiply(c, part, [t, t_left, t_right])
    gather_far(c, part)
    multiply(c, part, [t_far])
    finish(part)

    for c in range(CHUNKS):
        pltpu.make_async_copy(sbuf.at[c], sbuf.at[c], p1_send.at[c]).wait()
        for part in range(SPLIT):
            delivered(c, part, p2_send).wait()
            for way in range(6):
                y_copy(way, c, part).wait_send()


def attention_kernel(qkv_ref, len_ref, bs_ref, out_ref, keys, values, context, out_sem):
    s = lax.axis_index("section")
    i = lax.axis_index("dp")
    blocks = [bs_ref[s, i * NB + k] for k in range(NB)]
    ranks = [sum((other < block).astype(jnp.int32) for other in blocks) for block in blocks]
    slots = [sum(k * (ranks[k] == r).astype(jnp.int32) for k in range(NB)) for r in range(NB)]
    ordered = [sum(blocks[k] * (ranks[k] == r).astype(jnp.int32) for k in range(NB)) for r in range(NB)]
    across = lax.broadcasted_iota(jnp.int32, (1, BLK), 1)
    down = lax.broadcasted_iota(jnp.int32, (BLK, 1), 0)
    key_docs = [slot_docs(bs_ref, len_ref, s, block, across) for block in ordered]
    slot_rows = [pl.ds(pl.multiple_of(slot * BLK, BLK), BLK) for slot in slots]
    for r in range(NB):
        keys[:, r * BLK:(r + 1) * BLK] = qkv_ref[slot_rows[r], GQ * HD:(GQ + 1) * HD].T
        values[r * BLK:(r + 1) * BLK] = qkv_ref[slot_rows[r], (GQ + 1) * HD:]
    factor = math.log2(math.e) / math.sqrt(HD)

    def attend(r, first):
        row_doc, row_pos = slot_docs(bs_ref, len_ref, s, ordered[r], down)
        key_doc = jnp.concatenate([key_docs[f][0] for f in range(first, r + 1)], axis=1)
        key_pos = jnp.concatenate([key_docs[f][1] for f in range(first, r + 1)], axis=1)
        seen = (row_doc == key_doc) & (key_pos <= row_pos)
        near = slice(first * BLK, (r + 1) * BLK)
        near_keys, near_values = keys[:, near], values[near]
        for head in range(0, GQ, GROUP):
            group = range(head, head + GROUP)
            scores = [
                jnp.dot(qkv_ref[slot_rows[r], h * HD:(h + 1) * HD], near_keys, preferred_element_type=jnp.float32)
                for h in group
            ]
            scores = [jnp.where(seen, value, -1e30) for value in scores]
            row_max = [jnp.max(value, axis=1, keepdims=True) for value in scores]
            probs = [jnp.exp2((value - top) * factor) for value, top in zip(scores, row_max)]
            totals = [jnp.sum(value, axis=1, keepdims=True) for value in probs]
            sums = [
                jnp.dot(value.astype(jnp.bfloat16), near_values, preferred_element_type=jnp.float32)
                for value in probs
            ]
            for h, value, total in zip(group, sums, totals):
                context[r, :, h * HD:(h + 1) * HD] = (value / total).astype(jnp.bfloat16)

    copies = []
    for r in range(NB):
        same = [(ordered[f] // NB == ordered[r] // NB).astype(jnp.int32) for f in range(r)]
        count = sum(same) if same else jnp.int32(0)
        for earlier in range(r + 1):
            pl.when(count == earlier)(functools.partial(attend, r, r - earlier))
        copies.append(pltpu.make_async_copy(context.at[r], out_ref.at[slot_rows[r]], out_sem.at[r]))
        copies[r].start()
    for copy in copies:
        copy.wait()


def attention(qkv, by_document, block_source):
    rows = NB * BLK
    vmem = pl.BlockSpec(memory_space=pltpu.VMEM)
    smem = pl.BlockSpec(memory_space=pltpu.SMEM)
    return pl.pallas_call(
        attention_kernel,
        out_shape=jax.ShapeDtypeStruct((rows, GQ * HD), jnp.bfloat16),
        in_specs=[vmem, smem, smem],
        out_specs=pl.BlockSpec(memory_space=pl.ANY),
        scratch_shapes=[
            pltpu.VMEM((HD, rows), jnp.bfloat16),
            pltpu.VMEM((rows, HD), jnp.bfloat16),
            pltpu.VMEM((NB, BLK, GQ * HD), jnp.bfloat16),
            pltpu.SemaphoreType.DMA((NB,)),
        ],
        compiler_params=pltpu.CompilerParams(vmem_limit_bytes=32 * 1024 * 1024),
        cost_estimate=pl.CostEstimate(
            flops=4 * GQ * rows * rows * HD, bytes_accessed=rows * COLS * 4, transcendentals=GQ * rows * rows),
    )(qkv, by_document, block_source)


def local(sections, tensors, acts, w_qkv, lengths, block_source):
    rows = NB * BLK
    by_document = lengths.transpose(0, 2, 1)
    vmem = pl.BlockSpec(memory_space=pltpu.VMEM)
    smem = pl.BlockSpec(memory_space=pltpu.SMEM)
    qkv = pl.pallas_call(
        functools.partial(exchange_kernel, sections, tensors),
        out_shape=jax.ShapeDtypeStruct((rows, COLS), jnp.bfloat16),
        in_specs=[pl.BlockSpec(memory_space=pltpu.HBM)] * 2 + [smem] * 2,
        out_specs=vmem,
        scratch_shapes=[
            pltpu.VMEM((CHUNKS, NB, BLK, FEAT), jnp.bfloat16),
            pltpu.VMEM((CHUNKS, 2, CHIPS, NB, ROWS, HALF), jnp.bfloat16),
            pltpu.VMEM((CHUNKS, SPLIT, REPL, SLOTS, ROWS, HALF), jnp.bfloat16),
            pltpu.VMEM((4, CHUNKS, SPLIT, 2, CHIPS, SLOTS, ROWS, HALF), jnp.bfloat16),
            pltpu.VMEM((D, COLS), jnp.bfloat16),
            pltpu.VMEM((rows, COLS), jnp.float32),
            pltpu.VMEM((rows, HB), jnp.float32),
            pltpu.VMEM((SPLIT, CHIPS, SLOTS, ROWS, HD), jnp.float32),
            pltpu.VMEM((SPLIT, CHIPS, SLOTS, ROWS, HD), jnp.float32),
            pltpu.SemaphoreType.DMA((CHUNKS,)),
            pltpu.SemaphoreType.DMA,
            pltpu.SemaphoreType.DMA((CHUNKS,)),
            pltpu.SemaphoreType.DMA((CHUNKS,)),
            pltpu.SemaphoreType.DMA((CHUNKS, SPLIT)),
            pltpu.SemaphoreType.DMA((CHUNKS, SPLIT)),
            pltpu.SemaphoreType.DMA((6, CHUNKS, SPLIT)),
            pltpu.SemaphoreType.DMA((6, CHUNKS, SPLIT)),
        ] + [pltpu.VMEM((REPL, NB, ROWS, HALF), jnp.bfloat16)] * CHUNKS,
        compiler_params=pltpu.CompilerParams(
            collective_id=0, has_side_effects=True, vmem_limit_bytes=VMEM_BYTES),
        cost_estimate=pl.CostEstimate(
            flops=2 * rows * D * COLS, bytes_accessed=D * COLS * 2 + rows * COLS * 4, transcendentals=0),
    )(acts[0, :, 0], w_qkv[0], by_document, block_source)
    return attention(qkv, by_document, block_source)[None]


def solution(mesh):
    placed = (P("section", None, "dp", None, "tensor"), P("section", None, "tensor"), P(), P())
    return jax.shard_map(
        functools.partial(local, mesh.shape["section"], mesh.shape["tensor"]),
        mesh=mesh, in_specs=placed, out_specs=P("section", "dp", "tensor"), check_vma=False,
    )
```
